32 devices in a mesh: row: 4 (over z), col: 8 (over y, x, core).
Axes of the slice: x: 2, y: 2, z: 4, core: 2. Of those that a mesh axis runs over, the one named last changes fastest.
Arguments:
- dens_real: float32 [8192, 8192], P('row', 'col'), as said below
- dens_imag: float32 [8192, 8192], P('row', 'col'), as said below
- upper_band: float32 [8192, 384], P('row'), may hold values from -0.3 to 0.3
- pattern: int32 [64, 2], P('row'), may hold values 0 or 1
Outputs:
- new_real: float32 [8192, 8192], P('row', 'col')
- new_imag: float32 [8192, 8192], P('row', 'col')
The draws below stay inside these ranges and needn't reach their ends.
Inputs may be any that keep to these rules, and one draw needn't show every extreme that they name: dens_real is symmetric. dens_imag is antisymmetric, with a zero diagonal.
All inputs are finite; a program needn't handle non-finite values. No bound on the sum of `pattern` on one device may be relied on, other than what follows from the above.
Results may differ from the reference program's by a relative error of at most 0.0001.
Values sent between devices are 32-bit elements; how exact they have to be, the bound alone decides.
No kernel may reach another device: no remote copies, remote signals or barrier semaphores. Data moves between devices by JAX's collectives and lax.ppermute only.
A program may use at most 192 MiB of HBM per device.

```python
import jax
import jax.numpy as jnp
from jax import lax

N = 8192
BS = 128
KB = 2
NB = 64


def draw_dens_real(key, part):
    normal_draw = jax.random.normal(jax.random.fold_in(key, 11), (N, N), jnp.float32)
    symmetric = (normal_draw + normal_draw.T) * 0.7071
    return symmetric


def draw_dens_imag(key, part):
    normal_draw = jax.random.normal(jax.random.fold_in(key, 21), (N, N), jnp.float32)
    antisym = (normal_draw - normal_draw.T) * 0.7071
    return antisym


def place_ends(entries, stream_key, low, high):
    longest = entries.shape.index(max(entries.shape))
    spots = []
    for shift in (0, 1):
        where = [jax.random.randint(jax.random.fold_in(stream_key, axis), (), 0, length) for axis, length in enumerate(entries.shape)]
        where[longest] = (where[longest] + shift) % entries.shape[longest]
        spots.append(tuple(where))
    return entries.at[spots[0]].set(low).at[spots[1]].set(high)


def level_of(key, shape, shards, low, top_value):
    factor_of, own = 1.0, jax.random.fold_in(key, 6)
    for axis_at, parts in shards:
        steps = jnp.exp(jax.random.uniform(jax.random.fold_in(own, axis_at), (parts,), jnp.float32, low / len(shards), top_value / len(shards)))
        factor_of = factor_of * jnp.repeat(steps, shape[axis_at] // parts).reshape([-1 if axis == axis_at else 1 for axis in range(len(shape))])
    return factor_of


def scatter_about(key, dims, deviation, reach, shards=(), held_as=jnp.bfloat16):
    array = jax.random.normal(key, dims, jnp.float32) * deviation
    if len(shards) > 0:
        array = level_of(key, dims, shards, -0.22, 0.18) * array
    return jnp.clip(array, min=-reach, max=reach).astype(held_as)


def setup_inputs(seed: int = 0) -> dict:
    keys = jax.random.split(jax.random.key(seed), 5)
    return {
        "dens_real": draw_dens_real(jax.random.fold_in(keys[4], 71), 0),
        "dens_imag": draw_dens_imag(jax.random.fold_in(keys[4], 71), 0),
        "upper_band": scatter_about(keys[2], (N, (KB + 1) * BS), 0.05, 0.3, ((0, 4),), jnp.float32),
        "pattern": place_ends((jax.random.randint(keys[3], (NB, KB), 0, 5) < 3).astype(jnp.int32), jax.random.fold_in(keys[3], 1), 0, 1),
    }


HIGHEST_PRECISION = lax.Precision.HIGHEST
STEP_TIME = 0.3


def masked_band(upper_band, pattern, first_block):
    block_count = pattern.shape[0]
    blocks = upper_band.reshape(block_count, BS, KB + 1, BS)
    block_index = first_block + jnp.arange(block_count, dtype=jnp.int32)
    offsets = jnp.arange(1, KB + 1, dtype=jnp.int32)
    present = (pattern > 0) & (block_index[:, None] + offsets[None, :] < NB)
    factor = jnp.concatenate([jnp.ones((block_count, 1), jnp.float32), present.astype(jnp.float32)], axis=1)
    return (blocks * factor[:, None, :, None]).reshape(block_count * BS, (KB + 1) * BS)


def build_tiles(masked_ext, block_count):
    blocks = masked_ext.reshape(block_count + KB, BS, KB + 1, BS)
    tile_list = []
    for k in range(2 * KB + 1):
        offset_block = k - KB
        if offset_block < 0:
            distance = -offset_block
            piece_rows = blocks[KB - distance:KB - distance + block_count, :, distance, :]
            tile_list.append(jnp.swapaxes(piece_rows, 1, 2))
        elif offset_block == 0:
            piece_rows = blocks[KB:, :, 0, :]
            tile_list.append(0.5 * (piece_rows + jnp.swapaxes(piece_rows, 1, 2)))
        else:
            tile_list.append(blocks[KB:, :, offset_block, :])
    return jnp.stack(tile_list, axis=2)


def row_product(tile_set, rows_ext):
    block_count = tile_set.shape[0]
    stacked = rows_ext.reshape(block_count + 2 * KB, BS, rows_ext.shape[1])
    summed = jnp.einsum("jab,jbn->jan", tile_set[:, :, 0, :], stacked[0:block_count], precision=HIGHEST_PRECISION)
    for k in range(1, 2 * KB + 1):
        summed = summed + jnp.einsum("jab,jbn->jan", tile_set[:, :, k, :], stacked[k:k + block_count], precision=HIGHEST_PRECISION)
    return summed.reshape(block_count * BS, rows_ext.shape[1])


def column_product(tile_set, columns_ext):
    block_count = tile_set.shape[0]
    row_total = columns_ext.shape[0]
    stacked = columns_ext.reshape(row_total, block_count + 2 * KB, BS)
    summed = jnp.einsum("njb,jcb->njc", stacked[:, 0:block_count], tile_set[:, :, 0, :], precision=HIGHEST_PRECISION)
    for k in range(1, 2 * KB + 1):
        summed = summed + jnp.einsum("njb,jcb->njc", stacked[:, k:k + block_count], tile_set[:, :, k, :], precision=HIGHEST_PRECISION)
    return summed.reshape(row_total, block_count * BS)


def derivative(real_part, imag_part, tile_set):
    rim_width = KB * BS
    real_rows = jnp.pad(real_part, ((rim_width, rim_width), (0, 0)))
    imag_rows = jnp.pad(imag_part, ((rim_width, rim_width), (0, 0)))
    real_columns = jnp.pad(real_part, ((0, 0), (rim_width, rim_width)))
    imag_columns = jnp.pad(imag_part, ((0, 0), (rim_width, rim_width)))
    h_real = row_product(tile_set, real_rows)
    h_imag = row_product(tile_set, imag_rows)
    real_h = column_product(tile_set, real_columns)
    imag_h = column_product(tile_set, imag_columns)
    return h_imag - imag_h, real_h - h_real


def reference(dens_real, dens_imag, upper_band, pattern):
    masked = masked_band(upper_band, pattern, 0)
    masked_ext = jnp.pad(masked, ((KB * BS, 0), (0, 0)))
    tile_set = build_tiles(masked_ext, NB)
    first_real, first_imag = derivative(dens_real, dens_imag, tile_set)
    section_real = dens_real + STEP_TIME * first_real
    section_imag = dens_imag + STEP_TIME * first_imag
    second_real, second_imag = derivative(section_real, section_imag, tile_set)
    new_real = dens_real + 0.5 * STEP_TIME * (first_real + second_real)
    new_imag = dens_imag + 0.5 * STEP_TIME * (first_imag + second_imag)
    return new_real, new_imag
```

```python
import functools

import jax
import jax.numpy as jnp
from jax import lax
from jax.experimental import pallas as pl
from jax.experimental.pallas import tpu as pltpu
from jax.sharding import PartitionSpec as P

BS = 128
KB = 2
G = KB * BS
STEP_TIME = 0.3
F32 = jnp.float32
BF16 = jnp.bfloat16


def split(x):
    high = x.astype(BF16)
    low = (x - high.astype(F32)).astype(BF16)
    return high, low


def dot(a, b):
    return jnp.dot(a, b, preferred_element_type=F32)


def three(a_high, a_low, b_high, b_low):
    return dot(
        jnp.concatenate([a_high, a_low, a_high], axis=1),
        jnp.concatenate([b_high, b_high, b_low], axis=0),
    )


def band_kernel(transposed, u_ref, high_ref, low_ref):
    g = pl.program_id(0)
    first = pl.multiple_of(g * G, G)

    def upper(block, d):
        return u_ref[pl.ds(first + block * BS, BS), d * BS : (d + 1) * BS]

    for i in range(KB):
        for j in range(3 * KB):
            distance = (j - KB) - i
            if distance == 0:
                diag = upper(KB + i, 0)
                value = 0.5 * (diag + diag.T)
            elif 0 < distance <= KB:
                value = upper(KB + i, distance)
                value = value.T if transposed else value
            elif -KB <= distance < 0:
                value = upper(j, -distance)
                value = value if transposed else value.T
            else:
                value = jnp.zeros((BS, BS), F32)
            high, low = split(value)
            if transposed:
                at = (0, pl.ds(j * BS, BS), pl.ds(i * BS, BS))
            else:
                slot = lax.rem(g + 2 + j // KB, 3)
                column = pl.multiple_of(slot * G + (j % KB) * BS, BS)
                at = (0, pl.ds(i * BS, BS), pl.ds(column, BS))
            high_ref[at] = high
            low_ref[at] = low


def band_groups(u_ext, transposed):
    groups = u_ext.shape[0] // G - 1
    shape = (3 * G, G) if transposed else (G, 3 * G)
    out = jax.ShapeDtypeStruct((groups,) + shape, BF16)
    block = pl.BlockSpec((1,) + shape, lambda g: (g, 0, 0))
    return pl.pallas_call(
        functools.partial(band_kernel, transposed),
        grid=(groups,),
        in_specs=[pl.BlockSpec(u_ext.shape, lambda g: (0, 0))],
        out_specs=[block, block],
        out_shape=[out, out],
        compiler_params=pltpu.CompilerParams(vmem_limit_bytes=40 << 20),
        name="band_cols" if transposed else "band_rows",
    )(u_ext)


def load_ring(t, groups, p_ref, q_ref, ring):
    ph, pl_, qh, ql = ring
    slot = lax.rem(t, 3)

    @pl.when(t == 0)
    def _():
        for ref in ring:
            ref[2] = jnp.zeros(ref.shape[1:], BF16)

    @pl.when(t < groups)
    def _():
        ph[slot], pl_[slot] = split(p_ref[...])
        qh[slot], ql[slot] = split(q_ref[...])

    @pl.when(t == groups)
    def _():
        for ref in ring:
            ref[slot] = jnp.zeros(ref.shape[1:], BF16)


def left_product(both, xh, xl, at):
    w = dot(both, xh[:, :, at].reshape(3 * G, G))
    return w[:G] + w[G:] + dot(both[:G], xl[:, :, at].reshape(3 * G, G))


def right_product(lhs, n, columns, ch_ref, cl_ref):
    lo, hi = max(n - 1, 0) * G, min(n + 2, columns) * G
    k0 = lo - (n - 1) * G
    rows = lhs(slice(lo, hi))
    band = slice(k0, k0 + hi - lo)
    return three(rows[: 2 * G], rows[2 * G :], ch_ref[n, band, :], cl_ref[n, band, :])


def left_kernel(groups, p_ref, q_ref, hh_ref, hl_ref, po_ref, qo_ref, *ring):
    t = pl.program_id(0)
    load_ring(t, groups, p_ref, q_ref, ring)

    @pl.when(t > 0)
    def _():
        ph, pl_, qh, ql = ring
        both = jnp.concatenate([hh_ref[0], hl_ref[0]], axis=0)
        for n in range(ph.shape[2] // G):
            at = slice(n * G, (n + 1) * G)
            po_ref[:, at] = left_product(both, ph, pl_, at)
            qo_ref[:, at] = left_product(both, qh, ql, at)


def outer_kernel(side, p_ref, q_ref, h_ref, l_ref, halo_ref, pi_ref, qi_ref,
                 po_ref, qo_ref, rim_ref, rows):
    height = p_ref.shape[0]
    tile_at, halo_at = (slice(G, 3 * G), slice(0, 2 * G)), (slice(0, G), slice(2 * G, 3 * G))

    for k, x_ref in enumerate((p_ref, q_ref)):
        for half, value in enumerate(split(x_ref[...])):
            rows[k + 2 * half, :, tile_at[side]] = value
        for half, value in enumerate(split(halo_ref[k])):
            rows[k + 2 * half, :, halo_at[side]] = value
    high = rows[:2].reshape(2 * height, 3 * G)
    low = rows[2:].reshape(2 * height, 3 * G)
    right = three(high, low, h_ref[0], l_ref[0])
    p = pi_ref[...] - right[:height]
    q = qi_ref[...] - right[height:]
    po_ref[...] = p
    qo_ref[...] = q
    rim_ref[0], rim_ref[1] = p, q


def outer_columns(side, p, q, col_band, halo, p_left, q_left):
    height, width = p.shape
    rows = min(height, 2 * G)
    count, columns = height // rows, width // G
    band = pl.BlockSpec((1, 3 * G, G), lambda i: (side * (columns - 1), 0, 0))
    wide = pl.BlockSpec((rows, 2 * G), lambda i: (i, side * (columns // 2 - 1)))
    tile = pl.BlockSpec((rows, G), lambda i: (i, side * (columns - 1)))
    rim = pl.BlockSpec((2, rows, G), lambda i: (0, i, 0))
    out = jax.ShapeDtypeStruct(p.shape, F32)
    return pl.pallas_call(
        functools.partial(outer_kernel, side),
        grid=(count,),
        in_specs=[wide, wide, band, band, rim, tile, tile],
        out_specs=[tile, tile, rim],
        out_shape=[out, out, jax.ShapeDtypeStruct(halo.shape, F32)],
        input_output_aliases={5: 0, 6: 1},
        scratch_shapes=[pltpu.VMEM((4, rows, 3 * G), BF16)],
        compiler_params=pltpu.CompilerParams(vmem_limit_bytes=56 << 20),
        cost_estimate=pl.CostEstimate(flops=0, bytes_accessed=0, transcendentals=0),
        name="outer_columns",
    )(p, q, *col_band, halo, p_left, q_left)


def middle_kernel(groups, p_ref, q_ref, ch_ref, cl_ref, pi_ref, qi_ref,
                  po_ref, qo_ref, top_ref, bottom_ref, rows):
    i = pl.program_id(0)
    for k, x_ref in enumerate((p_ref, q_ref)):
        rows[k], rows[k + 2] = split(x_ref[...])
    columns = rows.shape[2] // G
    outs = ((pi_ref, po_ref), (qi_ref, qo_ref))
    for n in range(columns):
        at = slice(n * G, (n + 1) * G)
        if 0 < n < columns - 1:
            right = right_product(
                lambda w: rows[:, :, w].reshape(4 * G, w.stop - w.start), n, columns, ch_ref, cl_ref
            )
            for k, (i_ref, o_ref) in enumerate(outs):
                o_ref[:, at] = i_ref[:, at] - right[k * G : (k + 1) * G]
        else:
            for i_ref, o_ref in outs:
                o_ref[:, at] = i_ref[:, at]

    @pl.when(i == 0)
    def _():
        top_ref[0], top_ref[1] = po_ref[...], qo_ref[...]

    @pl.when(i == groups - 1)
    def _():
        bottom_ref[0], bottom_ref[1] = po_ref[...], qo_ref[...]


def middle_columns(p, q, col_band, p_left, q_left):
    height, width = p.shape
    groups = height // G
    tile = pl.BlockSpec((G, width), lambda i: (i, 0))
    band = pl.BlockSpec(col_band[0].shape, lambda i: (0, 0, 0))
    rim = pl.BlockSpec((2, G, width), lambda i: (0, 0, 0))
    out = jax.ShapeDtypeStruct(p.shape, F32)
    rim_out = jax.ShapeDtypeStruct((2, G, width), F32)
    return pl.pallas_call(
        functools.partial(middle_kernel, groups),
        grid=(groups,),
        in_specs=[tile, tile, band, band, tile, tile],
        out_specs=[tile, tile, rim, rim],
        out_shape=[out, out, rim_out, rim_out],
        input_output_aliases={4: 0, 5: 1},
        scratch_shapes=[pltpu.VMEM((4, G, width), BF16)],
        compiler_params=pltpu.CompilerParams(vmem_limit_bytes=56 << 20),
        cost_estimate=pl.CostEstimate(flops=0, bytes_accessed=0, transcendentals=0),
        name="middle_columns",
    )(p, q, *col_band, p_left, q_left)


def last_kernel(groups, p_ref, q_ref, hh_ref, hl_ref, ch_ref, cl_ref, pf_ref, qf_ref, a_ref, b_ref,
                po_ref, qo_ref, *ring):
    t = pl.program_id(0)
    load_ring(t, groups, p_ref, q_ref, ring)

    @pl.when(t > 0)
    def _():
        ph, pl_, qh, ql = ring
        mid = lax.rem(t + 2, 3)
        columns = ph.shape[2] // G
        both = jnp.concatenate([hh_ref[0], hl_ref[0]], axis=0)
        for n in range(columns):
            at = slice(n * G, (n + 1) * G)
            right = right_product(
                lambda w: jnp.concatenate([x[mid, :, w] for x in (ph, qh, pl_, ql)], axis=0),
                n, columns, ch_ref, cl_ref,
            )
            half_square = 0.5 * STEP_TIME * STEP_TIME
            slope = left_product(both, ph, pl_, at) - right[:G]
            po_ref[:, at] = a_ref[:, at] + STEP_TIME * qf_ref[:, at] - half_square * slope
            slope = left_product(both, qh, ql, at) - right[G:]
            qo_ref[:, at] = b_ref[:, at] - STEP_TIME * pf_ref[:, at] - half_square * slope


def ring_specs(p, groups):
    width = p.shape[1]
    ahead = pl.BlockSpec((G, width), lambda t: (jnp.minimum(t, groups - 1), 0))
    behind = pl.BlockSpec((G, width), lambda t: (jnp.maximum(t - 1, 0), 0))
    band = pl.BlockSpec((1, G, 3 * G), lambda t: (jnp.maximum(t - 1, 0), 0, 0))
    return ahead, behind, band, [pltpu.VMEM((3, G, width), BF16)] * 4


def from_left(p, q, row_band):
    groups = p.shape[0] // G
    ahead, behind, band, ring = ring_specs(p, groups)
    out = jax.ShapeDtypeStruct(p.shape, F32)
    return pl.pallas_call(
        functools.partial(left_kernel, groups),
        grid=(groups + 1,),
        in_specs=[ahead, ahead, band, band],
        out_specs=[behind, behind],
        out_shape=[out, out],
        scratch_shapes=ring,
        compiler_params=pltpu.CompilerParams(vmem_limit_bytes=56 << 20),
        cost_estimate=pl.CostEstimate(flops=0, bytes_accessed=0, transcendentals=0),
        name="from_left",
    )(p, q, *row_band)


def inner(p, q, row_band, col_band, a, b):
    groups = p.shape[0] // G
    ahead, behind, band, ring = ring_specs(p, groups)
    whole = pl.BlockSpec(col_band[0].shape, lambda t: (0, 0, 0))
    out = jax.ShapeDtypeStruct(p.shape, F32)
    return pl.pallas_call(
        functools.partial(last_kernel, groups),
        grid=(groups + 1,),
        in_specs=[ahead, ahead, band, band, whole, whole] + [behind] * 4,
        out_specs=[behind, behind],
        out_shape=[out, out],
        scratch_shapes=ring,
        compiler_params=pltpu.CompilerParams(vmem_limit_bytes=56 << 20),
        cost_estimate=pl.CostEstimate(flops=0, bytes_accessed=0, transcendentals=0),
        name="inner",
    )(p, q, *row_band, *col_band, p, q, a, b)


def row_edge_kernel(scale, h_ref, l_ref, above_ref, below_ref, p_ref, q_ref, *refs):
    outs, rims = (refs[1:3], refs[3:]) if len(refs) > 2 else (refs, ())
    high, low = h_ref[0], l_ref[0]
    both = jnp.concatenate([high, low], axis=0)

    def add(halo_ref):
        for k, (x_ref, o_ref) in enumerate(zip((p_ref, q_ref), outs)):
            xh, xl = split(halo_ref[k])
            w = dot(both, xh)
            value = x_ref[...] + scale * (w[:G] + w[G:] + dot(high, xl))
            o_ref[...] = value
            for rim in rims:
                rim[k] = value[:, :G]

    pl.when(pl.program_id(0) == 0)(lambda: add(above_ref))
    pl.when(pl.program_id(0) == 1)(lambda: add(below_ref))


def row_edges(p, q, above, below, edge_band, scale, rims=()):
    height, width = p.shape
    groups = height // G
    band = pl.BlockSpec((1, G, G), lambda s: (s, 0, 0))
    halo = pl.BlockSpec(above.shape, lambda s: (0, 0, 0))
    tile = pl.BlockSpec((G, width), lambda s: (s * (groups - 1), 0))
    rim = pl.BlockSpec((2, G, G), lambda s: (0, s * (groups - 1), 0))
    out = jax.ShapeDtypeStruct(p.shape, F32)
    return pl.pallas_call(
        functools.partial(row_edge_kernel, scale),
        grid=(2,),
        in_specs=[band, band, halo, halo, tile, tile] + [rim for _ in rims],
        out_specs=[tile, tile] + [rim for _ in rims],
        out_shape=[out, out] + [jax.ShapeDtypeStruct(x.shape, F32) for x in rims],
        input_output_aliases={4 + k: k for k in range(2 + len(rims))},
        compiler_params=pltpu.CompilerParams(vmem_limit_bytes=40 << 20),
        name="row_edges",
    )(*edge_band, above, below, p, q, *rims)


def col_edge_kernel(scale, relayed, with_rim, use_ref, *refs):
    h_ref, l_ref, before_ref, after_ref = refs[:4]
    refs = refs[4:]
    if relayed:
        extra_ref, refs = refs[0], refs[1:]
    p_ref, q_ref, po_ref, qo_ref = refs[:4]
    rim = refs[4:]
    s = pl.program_id(0)
    high, low = h_ref[0], l_ref[0]

    def add(halo_ref, side):
        rows = halo_ref.shape[1]
        halo = halo_ref[...].reshape(2 * rows, G)
        if relayed:
            halo = jnp.where(use_ref[side] > 0, extra_ref[...].reshape(2 * rows, G), halo)
        xh, xl = split(halo)
        w = dot(jnp.concatenate([xh, xl], axis=0), high)
        w = w[: 2 * rows] + w[2 * rows :] + dot(xh, low)
        for k, (x_ref, o_ref) in enumerate(((p_ref, po_ref), (q_ref, qo_ref))):
            value = x_ref[...] - scale * w[k * rows : (k + 1) * rows]
            o_ref[...] = value
            if with_rim:
                rim[side][k] = value

    pl.when(s == 0)(lambda: add(before_ref, 0))
    pl.when(s == 1)(lambda: add(after_ref, 1))


def col_edges(p, q, halos, edge_band, scale, use, groups, with_rim):
    before, after, extra = halos
    width = p.shape[1]
    first, step, count = groups
    columns = width // G
    rows = G
    if first == 0 and step == 1:
        rows = before.shape[1] // 4
        count = 4
    band = pl.BlockSpec((1, G, G), lambda s, i, use: (s, 0, 0))
    tile = pl.BlockSpec((rows, G), lambda s, i, use: (first + i * step, s * (columns - 1)))
    left = pl.BlockSpec((2, rows, G), lambda s, i, use: (0, jnp.where(s == 0, i, count - 1), 0))
    right = pl.BlockSpec((2, rows, G), lambda s, i, use: (0, jnp.where(s == 0, 0, i), 0))
    other = pl.BlockSpec((2, rows, G), lambda s, i, use: (0, i * use[s], 0))
    relayed = extra is not None
    out = jax.ShapeDtypeStruct(p.shape, F32)
    rim = jax.ShapeDtypeStruct(before.shape, F32)
    base = 5 + relayed
    return pl.pallas_call(
        functools.partial(col_edge_kernel, scale, relayed, with_rim),
        grid_spec=pltpu.PrefetchScalarGridSpec(
            num_scalar_prefetch=1,
            grid=(2, count),
            in_specs=[band, band, left, right] + [other] * relayed + [tile, tile],
            out_specs=[tile, tile] + ([left, right] if with_rim else []),
        ),
        out_shape=[out, out] + ([rim, rim] if with_rim else []),
        input_output_aliases={base: 0, base + 1: 1},
        compiler_params=pltpu.CompilerParams(vmem_limit_bytes=40 << 20),
        name="col_edges",
    )(use, *edge_band, before, after, *([extra] if relayed else []), p, q)


def chain(devices, by):
    return [(i, i + by) for i in range(devices) if 0 <= i + by < devices]


def swap_row_rims(top, bottom):
    devices = lax.axis_size("row")
    above = lax.ppermute(bottom, "row", chain(devices, 1))
    below = lax.ppermute(top, "row", chain(devices, -1))
    return above, below


def swap_col_rims(left, right, relayed):
    devices = lax.axis_size("col")
    half = devices // 2
    up, down = chain(devices, 1), chain(devices, -1)
    extra = None
    if relayed:
        up.remove((half - 1, half))
        down.remove((half, half - 1))
        mine = jnp.where(lax.axis_index("col") == half - 1, right, left)
        there = lax.ppermute(mine, "col", [(half - 1, devices - 1), (half, 0)])
    before = lax.ppermute(right, "col", up)
    after = lax.ppermute(left, "col", down)
    if relayed:
        extra = lax.ppermute(there, "col", [(devices - 1, half), (0, half - 1)])
    return before, after, extra


def masked_rows(upper_band, pattern, first_block, block_total):
    height, width = upper_band.shape
    count = height // BS
    block = first_block + jnp.arange(count, dtype=jnp.int32)
    offset = lax.broadcasted_iota(jnp.int32, (count, BS, width), 2) // BS
    factor = jnp.ones((count, BS, width), F32)
    for d in range(1, KB + 1):
        present = (pattern[:, d - 1] > 0) & (block + d < block_total)
        factor = jnp.where(offset == d, present.astype(F32)[:, None, None], factor)
    return (upper_band.reshape(count, BS, width) * factor).reshape(height, width)


def spread(value, axis, source):
    kept = jnp.where(lax.axis_index(axis) == source, value, 0).astype(value.dtype)
    return lax.psum(kept, axis)


def after(first, *values):
    return lax.optimization_barrier((first, *values))[1:]


def column_panel(panel, width, meanwhile):
    row_devices, col_devices = lax.axis_size("row"), lax.axis_size("col")
    row, col = lax.axis_index("row"), lax.axis_index("col")
    per_row = col_devices // row_devices
    if (row_devices, col_devices) != (4, 8):
        source = col // per_row
        whole = spread(panel, "row", source)
        return lax.dynamic_slice_in_dim(whole, (col - source * per_row) * width, width + G, 0), panel, panel[:G]
    y, x, k = col // 4, (col // 2) % 2, col % 2
    rows = (width + G) // 2
    own = lax.dynamic_slice_in_dim(panel, k * width + y * rows, rows, 0)
    cols = lambda side: [c for c in range(col_devices) if (c // 2) % 2 == side]
    pairs = lambda hops: [
        (r * col_devices + c, t * col_devices + c) for side, r, t in hops for c in cols(side)
    ]
    both = ("row", "col")
    far = lax.ppermute(own, both, pairs([(0, 0, 2), (0, 2, 0), (1, 1, 3), (1, 3, 1)]))
    up = lax.ppermute(own, both, pairs([(0, 0, 1), (0, 2, 3), (1, 1, 2)]))
    down = lax.ppermute(own, both, pairs([(0, 2, 1), (1, 1, 0), (1, 3, 2)]))
    far, up, down = after(meanwhile, far, up, down)
    last = lax.ppermute(far, both, pairs([(0, 2, 3), (1, 1, 0)]))
    at = row - x
    low = jnp.where(at == -1, down, jnp.where(at == 0, own, jnp.where(at == 1, up, jnp.where((at == 2), far, last))))
    high = jnp.where(at == 2, own, jnp.where(at == 1, down, jnp.where(at == 3, up, jnp.where(at == 0, far, last))))
    mine, other = jnp.where(y == 0, low, high), jnp.where(y == 0, high, low)
    got = lax.ppermute(other, "col", [(c, (c + 4) % 8) for c in range(8)])
    parts = [jnp.where(y == 0, mine, got), jnp.where(y == 0, got, mine)]
    return jnp.concatenate(parts, axis=0), last, own


def shards(dens_real, dens_imag, upper_band, pattern):
    height, width = dens_real.shape
    row_blocks = height // BS
    row_devices, col_devices = lax.axis_size("row"), lax.axis_size("col")
    row, col = lax.axis_index("row"), lax.axis_index("col")
    first, total = row * row_blocks, row_blocks * row_devices
    tail = masked_rows(upper_band[-G:], pattern[-KB:], first + row_blocks - KB, total)
    above = lax.ppermute(tail[:, BS:], "row", chain(row_devices, 1))
    masked = masked_rows(upper_band, pattern, first, total)
    panel = jnp.concatenate([jnp.pad(above, ((0, 0), (BS, 0))), masked], axis=0)
    row_band = band_groups(panel, False)
    real, imag = dens_real, dens_imag
    x_real, x_imag = from_left(real, imag, row_band)
    own_panel, landed, own_part = column_panel(panel, width, x_real)
    col_band = band_groups(own_panel, True)

    groups, columns = height // G, width // G
    slot_above, slot_below = 2, groups % 3

    def row_edge(x):
        return jnp.stack(
            [
                x[0, :, slot_above * G : (slot_above + 1) * G],
                x[groups - 1, :, slot_below * G : (slot_below + 1) * G],
            ]
        )

    def col_edge(x):
        return jnp.stack([x[0, :G], x[columns - 1, 2 * G :]])

    row_edge_band = [row_edge(x) for x in row_band]
    col_edge_band = [col_edge(x) for x in col_band]
    half = col_devices // 2
    use = jnp.stack([col == half, col == half - 1]).astype(jnp.int32)

    rim_left = jnp.stack([real[:, :G], imag[:, :G]])
    rim_right = jnp.stack([real[:, -G:], imag[:, -G:]])
    before, behind, _ = swap_col_rims(*after(own_part, rim_left, rim_right), False)
    top, bottom = jnp.stack([real[:G], imag[:G]]), jnp.stack([real[-G:], imag[-G:]])
    above, below = swap_row_rims(*after(landed, top, bottom))
    x_real, x_imag, left = outer_columns(0, real, imag, col_band, before, x_real, x_imag)
    x_real, x_imag, left = row_edges(
        x_real, x_imag, above, below, row_edge_band, 1.0, (left,)
    )
    next_after = lax.ppermute(left, "col", chain(col_devices, -1))
    x_real, x_imag, right = outer_columns(1, real, imag, col_band, behind, x_real, x_imag)
    next_before = lax.ppermute(right, "col", chain(col_devices, 1))
    x_real, x_imag, top, bottom = middle_columns(real, imag, col_band, x_real, x_imag)
    above, below = swap_row_rims(top, bottom)

    scale = -0.5 * STEP_TIME * STEP_TIME
    new_real, new_imag = inner(x_real, x_imag, row_band, col_band, real, imag)
    new_real, new_imag = row_edges(new_real, new_imag, above, below, row_edge_band, scale)
    new_real, new_imag = col_edges(
        new_real, new_imag, (next_before, next_after, None), col_edge_band, scale, use, (0, 1, groups), False
    )
    return new_real, new_imag


def solution(mesh):
    in_specs = (P("row", "col"), P("row", "col"), P("row", None), P("row", None))
    out_specs = (P("row", "col"), P("row", "col"))
    return jax.shard_map(shards, mesh=mesh, in_specs=in_specs, out_specs=out_specs, check_vma=False)
```

```python
import functools

import jax
import jax.numpy as jnp
from jax import lax
from jax.experimental import pallas as pl
from jax.experimental.pallas import tpu as pltpu
from jax.sharding import PartitionSpec as P

BS = 128
KB = 2
G = KB * BS
STEP_TIME = 0.3
F32 = jnp.float32
BF16 = jnp.bfloat16


def split(x):
    high = x.astype(BF16)
    low = (x - high.astype(F32)).astype(BF16)
    return high, low


def dot(a, b):
    return jnp.dot(a, b, preferred_element_type=F32)


def three(a_high, a_low, b_high, b_low):
    return dot(
        jnp.concatenate([a_high, a_low, a_high], axis=1),
        jnp.concatenate([b_high, b_high, b_low], axis=0),
    )


def band_kernel(transposed, u_ref, high_ref, low_ref):
    g = pl.program_id(0)
    first = pl.multiple_of(g * G, G)

    def upper(block, d):
        return u_ref[pl.ds(first + block * BS, BS), d * BS : (d + 1) * BS]

    for i in range(KB):
        for j in range(3 * KB):
            distance = (j - KB) - i
            if distance == 0:
                diag = upper(KB + i, 0)
                value = 0.5 * (diag + diag.T)
            elif 0 < distance <= KB:
                value = upper(KB + i, distance)
                value = value.T if transposed else value
            elif -KB <= distance < 0:
                value = upper(j, -distance)
                value = value if transposed else value.T
            else:
                value = jnp.zeros((BS, BS), F32)
            high, low = split(value)
            if transposed:
                at = (0, pl.ds(j * BS, BS), pl.ds(i * BS, BS))
            else:
                slot = lax.rem(g + 2 + j // KB, 3)
                column = pl.multiple_of(slot * G + (j % KB) * BS, BS)
                at = (0, pl.ds(i * BS, BS), pl.ds(column, BS))
            high_ref[at] = high
            low_ref[at] = low


def band_groups(u_ext, transposed):
    groups = u_ext.shape[0] // G - 1
    shape = (3 * G, G) if transposed else (G, 3 * G)
    out = jax.ShapeDtypeStruct((groups,) + shape, BF16)
    block = pl.BlockSpec((1,) + shape, lambda g: (g, 0, 0))
    return pl.pallas_call(
        functools.partial(band_kernel, transposed),
        grid=(groups,),
        in_specs=[pl.BlockSpec(u_ext.shape, lambda g: (0, 0))],
        out_specs=[block, block],
        out_shape=[out, out],
        compiler_params=pltpu.CompilerParams(vmem_limit_bytes=40 << 20),
        name="band_cols" if transposed else "band_rows",
    )(u_ext)


def load_ring(t, groups, p_ref, q_ref, ring):
    ph, pl_, qh, ql = ring
    slot = lax.rem(t, 3)

    @pl.when(t == 0)
    def _():
        for ref in ring:
            ref[2] = jnp.zeros(ref.shape[1:], BF16)

    @pl.when(t < groups)
    def _():
        ph[slot], pl_[slot] = split(p_ref[...])
        qh[slot], ql[slot] = split(q_ref[...])

    @pl.when(t == groups)
    def _():
        for ref in ring:
            ref[slot] = jnp.zeros(ref.shape[1:], BF16)


def left_product(both, xh, xl, at):
    w = dot(both, xh[:, :, at].reshape(3 * G, G))
    return w[:G] + w[G:] + dot(both[:G], xl[:, :, at].reshape(3 * G, G))


def right_product(lhs, n, columns, ch_ref, cl_ref):
    lo, hi = max(n - 1, 0) * G, min(n + 2, columns) * G
    k0 = lo - (n - 1) * G
    rows = lhs(slice(lo, hi))
    band = slice(k0, k0 + hi - lo)
    return three(rows[: 2 * G], rows[2 * G :], ch_ref[n, band, :], cl_ref[n, band, :])


def left_kernel(groups, p_ref, q_ref, hh_ref, hl_ref, po_ref, qo_ref, *ring):
    t = pl.program_id(0)
    load_ring(t, groups, p_ref, q_ref, ring)

    @pl.when(t > 0)
    def _():
        ph, pl_, qh, ql = ring
        both = jnp.concatenate([hh_ref[0], hl_ref[0]], axis=0)
        for n in range(ph.shape[2] // G):
            at = slice(n * G, (n + 1) * G)
            po_ref[:, at] = left_product(both, ph, pl_, at)
            qo_ref[:, at] = left_product(both, qh, ql, at)


def outer_kernel(side, p_ref, q_ref, h_ref, l_ref, halo_ref, pi_ref, qi_ref,
                 po_ref, qo_ref, rim_ref, rows):
    height = p_ref.shape[0]
    tile_at, halo_at = (slice(G, 3 * G), slice(0, 2 * G)), (slice(0, G), slice(2 * G, 3 * G))

    for k, x_ref in enumerate((p_ref, q_ref)):
        for half, value in enumerate(split(x_ref[...])):
            rows[k + 2 * half, :, tile_at[side]] = value
        for half, value in enumerate(split(halo_ref[k])):
            rows[k + 2 * half, :, halo_at[side]] = value
    high = rows[:2].reshape(2 * height, 3 * G)
    low = rows[2:].reshape(2 * height, 3 * G)
    right = three(high, low, h_ref[0], l_ref[0])
    p = pi_ref[...] - right[:height]
    q = qi_ref[...] - right[height:]
    po_ref[...] = p
    qo_ref[...] = q
    rim_ref[0], rim_ref[1] = p, q


def outer_columns(side, p, q, col_band, halo, p_left, q_left):
    height, width = p.shape
    rows = min(height, 2 * G)
    count, columns = height // rows, width // G
    band = pl.BlockSpec((1, 3 * G, G), lambda i: (side * (columns - 1), 0, 0))
    wide = pl.BlockSpec((rows, 2 * G), lambda i: (i, side * (columns // 2 - 1)))
    tile = pl.BlockSpec((rows, G), lambda i: (i, side * (columns - 1)))
    rim = pl.BlockSpec((2, rows, G), lambda i: (0, i, 0))
    out = jax.ShapeDtypeStruct(p.shape, F32)
    return pl.pallas_call(
        functools.partial(outer_kernel, side),
        grid=(count,),
        in_specs=[wide, wide, band, band, rim, tile, tile],
        out_specs=[tile, tile, rim],
        out_shape=[out, out, jax.ShapeDtypeStruct(halo.shape, F32)],
        input_output_aliases={5: 0, 6: 1},
        scratch_shapes=[pltpu.VMEM((4, rows, 3 * G), BF16)],
        compiler_params=pltpu.CompilerParams(vmem_limit_bytes=56 << 20),
        cost_estimate=pl.CostEstimate(flops=0, bytes_accessed=0, transcendentals=0),
        name="outer_columns",
    )(p, q, *col_band, halo, p_left, q_left)


def middle_kernel(columns, p_ref, q_ref, ch_ref, cl_ref, pi_ref, qi_ref, po_ref, qo_ref, rows):
    n = pl.program_id(1)
    height = p_ref.shape[0]

    @pl.when(n == 0)
    def _():
        for k, x_ref in enumerate((p_ref, q_ref)):
            rows[k], rows[k + 2] = split(x_ref[...])

    def product(at):
        window = slice((at - 1) * G, (at + 2) * G)
        high = rows[:2, :, window].reshape(2 * height, 3 * G)
        low = rows[2:, :, window].reshape(2 * height, 3 * G)
        right = three(high, low, ch_ref[at], cl_ref[at])
        po_ref[...] = pi_ref[...] - right[:height]
        qo_ref[...] = qi_ref[...] - right[height:]

    for at in range(1, columns - 1):
        pl.when(n == at - 1)(functools.partial(product, at))


def middle_columns(p, q, col_band, p_left, q_left):
    height, width = p.shape
    columns = width // G
    if columns <= 2:
        return p_left, q_left
    rows = min(height, 2 * G)
    whole = pl.BlockSpec((rows, width), lambda i, n: (i, 0))
    band = pl.BlockSpec(col_band[0].shape, lambda i, n: (0, 0, 0))
    tile = pl.BlockSpec((rows, G), lambda i, n: (i, n + 1))
    out = jax.ShapeDtypeStruct(p.shape, F32)
    return pl.pallas_call(
        functools.partial(middle_kernel, columns),
        grid=(height // rows, columns - 2),
        in_specs=[whole, whole, band, band, tile, tile],
        out_specs=[tile, tile],
        out_shape=[out, out],
        input_output_aliases={4: 0, 5: 1},
        scratch_shapes=[pltpu.VMEM((4, rows, width), BF16)],
        compiler_params=pltpu.CompilerParams(vmem_limit_bytes=56 << 20),
        cost_estimate=pl.CostEstimate(flops=0, bytes_accessed=0, transcendentals=0),
        name="middle_columns",
    )(p, q, *col_band, p_left, q_left)


def last_kernel(groups, p_ref, q_ref, hh_ref, hl_ref, ch_ref, cl_ref, pf_ref, qf_ref, a_ref, b_ref,
                po_ref, qo_ref, *ring):
    t = pl.program_id(0)
    load_ring(t, groups, p_ref, q_ref, ring)

    @pl.when(t > 0)
    def _():
        ph, pl_, qh, ql = ring
        mid = lax.rem(t + 2, 3)
        columns = ph.shape[2] // G
        both = jnp.concatenate([hh_ref[0], hl_ref[0]], axis=0)
        for n in range(columns):
            at = slice(n * G, (n + 1) * G)
            right = right_product(
                lambda w: jnp.concatenate([x[mid, :, w] for x in (ph, qh, pl_, ql)], axis=0),
                n, columns, ch_ref, cl_ref,
            )
            half_square = 0.5 * STEP_TIME * STEP_TIME
            slope = left_product(both, ph, pl_, at) - right[:G]
            po_ref[:, at] = a_ref[:, at] + STEP_TIME * qf_ref[:, at] - half_square * slope
            slope = left_product(both, qh, ql, at) - right[G:]
            qo_ref[:, at] = b_ref[:, at] - STEP_TIME * pf_ref[:, at] - half_square * slope


def ring_specs(p, groups):
    width = p.shape[1]
    ahead = pl.BlockSpec((G, width), lambda t: (jnp.minimum(t, groups - 1), 0))
    behind = pl.BlockSpec((G, width), lambda t: (jnp.maximum(t - 1, 0), 0))
    band = pl.BlockSpec((1, G, 3 * G), lambda t: (jnp.maximum(t - 1, 0), 0, 0))
    return ahead, behind, band, [pltpu.VMEM((3, G, width), BF16)] * 4


def from_left(p, q, row_band):
    groups = p.shape[0] // G
    ahead, behind, band, ring = ring_specs(p, groups)
    out = jax.ShapeDtypeStruct(p.shape, F32)
    return pl.pallas_call(
        functools.partial(left_kernel, groups),
        grid=(groups + 1,),
        in_specs=[ahead, ahead, band, band],
        out_specs=[behind, behind],
        out_shape=[out, out],
        scratch_shapes=ring,
        compiler_params=pltpu.CompilerParams(vmem_limit_bytes=56 << 20),
        cost_estimate=pl.CostEstimate(flops=0, bytes_accessed=0, transcendentals=0),
        name="from_left",
    )(p, q, *row_band)


def inner(p, q, row_band, col_band, a, b):
    groups = p.shape[0] // G
    ahead, behind, band, ring = ring_specs(p, groups)
    whole = pl.BlockSpec(col_band[0].shape, lambda t: (0, 0, 0))
    out = jax.ShapeDtypeStruct(p.shape, F32)
    return pl.pallas_call(
        functools.partial(last_kernel, groups),
        grid=(groups + 1,),
        in_specs=[ahead, ahead, band, band, whole, whole] + [behind] * 4,
        out_specs=[behind, behind],
        out_shape=[out, out],
        scratch_shapes=ring,
        compiler_params=pltpu.CompilerParams(vmem_limit_bytes=56 << 20),
        cost_estimate=pl.CostEstimate(flops=0, bytes_accessed=0, transcendentals=0),
        name="inner",
    )(p, q, *row_band, *col_band, p, q, a, b)


def row_edge_kernel(scale, h_ref, l_ref, above_ref, below_ref, p_ref, q_ref, *refs):
    outs, rims = (refs[1:3], refs[3:]) if len(refs) > 2 else (refs, ())
    high, low = h_ref[0], l_ref[0]
    both = jnp.concatenate([high, low], axis=0)

    def add(halo_ref):
        for k, (x_ref, o_ref) in enumerate(zip((p_ref, q_ref), outs)):
            xh, xl = split(halo_ref[k])
            w = dot(both, xh)
            value = x_ref[...] + scale * (w[:G] + w[G:] + dot(high, xl))
            o_ref[...] = value
            for rim in rims:
                rim[k] = value[:, :G]

    pl.when(pl.program_id(0) == 0)(lambda: add(above_ref))
    pl.when(pl.program_id(0) == 1)(lambda: add(below_ref))


def row_edges(p, q, above, below, edge_band, scale, rims=()):
    height, width = p.shape
    groups = height // G
    band = pl.BlockSpec((1, G, G), lambda s: (s, 0, 0))
    halo = pl.BlockSpec(above.shape, lambda s: (0, 0, 0))
    tile = pl.BlockSpec((G, width), lambda s: (s * (groups - 1), 0))
    rim = pl.BlockSpec((2, G, G), lambda s: (0, s * (groups - 1), 0))
    out = jax.ShapeDtypeStruct(p.shape, F32)
    return pl.pallas_call(
        functools.partial(row_edge_kernel, scale),
        grid=(2,),
        in_specs=[band, band, halo, halo, tile, tile] + [rim for _ in rims],
        out_specs=[tile, tile] + [rim for _ in rims],
        out_shape=[out, out] + [jax.ShapeDtypeStruct(x.shape, F32) for x in rims],
        input_output_aliases={4 + k: k for k in range(2 + len(rims))},
        compiler_params=pltpu.CompilerParams(vmem_limit_bytes=40 << 20),
        name="row_edges",
    )(*edge_band, above, below, p, q, *rims)


def col_edge_kernel(scale, relayed, with_rim, use_ref, *refs):
    h_ref, l_ref, before_ref, after_ref = refs[:4]
    refs = refs[4:]
    if relayed:
        extra_ref, refs = refs[0], refs[1:]
    p_ref, q_ref, po_ref, qo_ref = refs[:4]
    rim = refs[4:]
    s = pl.program_id(0)
    high, low = h_ref[0], l_ref[0]

    def add(halo_ref, side):
        rows = halo_ref.shape[1]
        halo = halo_ref[...].reshape(2 * rows, G)
        if relayed:
            halo = jnp.where(use_ref[side] > 0, extra_ref[...].reshape(2 * rows, G), halo)
        xh, xl = split(halo)
        w = dot(jnp.concatenate([xh, xl], axis=0), high)
        w = w[: 2 * rows] + w[2 * rows :] + dot(xh, low)
        for k, (x_ref, o_ref) in enumerate(((p_ref, po_ref), (q_ref, qo_ref))):
            value = x_ref[...] - scale * w[k * rows : (k + 1) * rows]
            o_ref[...] = value
            if with_rim:
                rim[side][k] = value

    pl.when(s == 0)(lambda: add(before_ref, 0))
    pl.when(s == 1)(lambda: add(after_ref, 1))


def col_edges(p, q, halos, edge_band, scale, use, groups, with_rim):
    before, after, extra = halos
    width = p.shape[1]
    first, step, count = groups
    columns = width // G
    rows = G
    if first == 0 and step == 1:
        rows = before.shape[1] // 4
        count = 4
    band = pl.BlockSpec((1, G, G), lambda s, i, use: (s, 0, 0))
    tile = pl.BlockSpec((rows, G), lambda s, i, use: (first + i * step, s * (columns - 1)))
    left = pl.BlockSpec((2, rows, G), lambda s, i, use: (0, jnp.where(s == 0, i, count - 1), 0))
    right = pl.BlockSpec((2, rows, G), lambda s, i, use: (0, jnp.where(s == 0, 0, i), 0))
    other = pl.BlockSpec((2, rows, G), lambda s, i, use: (0, i * use[s], 0))
    relayed = extra is not None
    out = jax.ShapeDtypeStruct(p.shape, F32)
    rim = jax.ShapeDtypeStruct(before.shape, F32)
    base = 5 + relayed
    return pl.pallas_call(
        functools.partial(col_edge_kernel, scale, relayed, with_rim),
        grid_spec=pltpu.PrefetchScalarGridSpec(
            num_scalar_prefetch=1,
            grid=(2, count),
            in_specs=[band, band, left, right] + [other] * relayed + [tile, tile],
            out_specs=[tile, tile] + ([left, right] if with_rim else []),
        ),
        out_shape=[out, out] + ([rim, rim] if with_rim else []),
        input_output_aliases={base: 0, base + 1: 1},
        compiler_params=pltpu.CompilerParams(vmem_limit_bytes=40 << 20),
        name="col_edges",
    )(use, *edge_band, before, after, *([extra] if relayed else []), p, q)


def chain(devices, by):
    return [(i, i + by) for i in range(devices) if 0 <= i + by < devices]


def swap_row_rims(top, bottom):
    devices = lax.axis_size("row")
    above = lax.ppermute(bottom, "row", chain(devices, 1))
    below = lax.ppermute(top, "row", chain(devices, -1))
    return above, below


def swap_col_rims(left, right, relayed):
    devices = lax.axis_size("col")
    half = devices // 2
    up, down = chain(devices, 1), chain(devices, -1)
    extra = None
    if relayed:
        up.remove((half - 1, half))
        down.remove((half, half - 1))
        mine = jnp.where(lax.axis_index("col") == half - 1, right, left)
        there = lax.ppermute(mine, "col", [(half - 1, devices - 1), (half, 0)])
    before = lax.ppermute(right, "col", up)
    after = lax.ppermute(left, "col", down)
    if relayed:
        extra = lax.ppermute(there, "col", [(devices - 1, half), (0, half - 1)])
    return before, after, extra


def masked_rows(upper_band, pattern, first_block, block_total):
    height, width = upper_band.shape
    count = height // BS
    block = first_block + jnp.arange(count, dtype=jnp.int32)
    offset = lax.broadcasted_iota(jnp.int32, (count, BS, width), 2) // BS
    factor = jnp.ones((count, BS, width), F32)
    for d in range(1, KB + 1):
        present = (pattern[:, d - 1] > 0) & (block + d < block_total)
        factor = jnp.where(offset == d, present.astype(F32)[:, None, None], factor)
    return (upper_band.reshape(count, BS, width) * factor).reshape(height, width)


def spread(value, axis, source):
    kept = jnp.where(lax.axis_index(axis) == source, value, 0).astype(value.dtype)
    return lax.psum(kept, axis)


def after(first, *values):
    return lax.optimization_barrier((first, *values))[1:]


def column_panel(panel, width, meanwhile):
    row_devices, col_devices = lax.axis_size("row"), lax.axis_size("col")
    row, col = lax.axis_index("row"), lax.axis_index("col")
    per_row = col_devices // row_devices
    if (row_devices, col_devices) != (4, 8):
        source = col // per_row
        whole = spread(panel, "row", source)
        return lax.dynamic_slice_in_dim(whole, (col - source * per_row) * width, width + G, 0), panel
    y, x, k = col // 4, (col // 2) % 2, col % 2
    rows = (width + G) // 2
    own = lax.dynamic_slice_in_dim(panel, k * width + y * rows, rows, 0)
    cols = lambda side: [c for c in range(col_devices) if (c // 2) % 2 == side]
    pairs = lambda hops: [
        (r * col_devices + c, t * col_devices + c) for side, r, t in hops for c in cols(side)
    ]
    both = ("row", "col")
    far = lax.ppermute(own, both, pairs([(0, 0, 2), (0, 2, 0), (1, 1, 3), (1, 3, 1)]))
    up = lax.ppermute(own, both, pairs([(0, 0, 1), (0, 2, 3), (1, 1, 2)]))
    down = lax.ppermute(own, both, pairs([(0, 2, 1), (1, 1, 0), (1, 3, 2)]))
    far, up, down = after(meanwhile, far, up, down)
    last = lax.ppermute(far, both, pairs([(0, 2, 3), (1, 1, 0)]))
    at = row - x
    low = jnp.where(at == -1, down, jnp.where(at == 0, own, jnp.where(at == 1, up, jnp.where((at == 2), far, last))))
    high = jnp.where(at == 2, own, jnp.where(at == 1, down, jnp.where(at == 3, up, jnp.where(at == 0, far, last))))
    mine, other = jnp.where(y == 0, low, high), jnp.where(y == 0, high, low)
    got = lax.ppermute(other, "col", [(c, (c + 4) % 8) for c in range(8)])
    parts = [jnp.where(y == 0, mine, got), jnp.where(y == 0, got, mine)]
    return jnp.concatenate(parts, axis=0), other


def shards(dens_real, dens_imag, upper_band, pattern):
    height, width = dens_real.shape
    row_blocks = height // BS
    row_devices, col_devices = lax.axis_size("row"), lax.axis_size("col")
    row, col = lax.axis_index("row"), lax.axis_index("col")
    first, total = row * row_blocks, row_blocks * row_devices
    tail = masked_rows(upper_band[-G:], pattern[-KB:], first + row_blocks - KB, total)
    above = lax.ppermute(tail[:, BS:], "row", chain(row_devices, 1))
    masked = masked_rows(upper_band, pattern, first, total)
    panel = jnp.concatenate([jnp.pad(above, ((0, 0), (BS, 0))), masked], axis=0)
    row_band = band_groups(panel, False)
    real, imag = dens_real, dens_imag
    x_real, x_imag = from_left(real, imag, row_band)
    own_panel, landed = column_panel(panel, width, x_real)
    col_band = band_groups(own_panel, True)

    groups, columns = height // G, width // G
    slot_above, slot_below = 2, groups % 3

    def row_edge(x):
        return jnp.stack(
            [
                x[0, :, slot_above * G : (slot_above + 1) * G],
                x[groups - 1, :, slot_below * G : (slot_below + 1) * G],
            ]
        )

    def col_edge(x):
        return jnp.stack([x[0, :G], x[columns - 1, 2 * G :]])

    row_edge_band = [row_edge(x) for x in row_band]
    col_edge_band = [col_edge(x) for x in col_band]
    half = col_devices // 2
    use = jnp.stack([col == half, col == half - 1]).astype(jnp.int32)

    rim_left = jnp.stack([real[:, :G], imag[:, :G]])
    rim_right = jnp.stack([real[:, -G:], imag[:, -G:]])
    before, behind, _ = swap_col_rims(rim_left, rim_right, False)
    top, bottom = jnp.stack([real[:G], imag[:G]]), jnp.stack([real[-G:], imag[-G:]])
    above, below = swap_row_rims(*after(landed, top, bottom))
    x_real, x_imag, left = outer_columns(0, real, imag, col_band, before, x_real, x_imag)
    x_real, x_imag, left = row_edges(
        x_real, x_imag, above, below, row_edge_band, 1.0, (left,)
    )
    next_after = lax.ppermute(left, "col", chain(col_devices, -1))
    x_real, x_imag, right = outer_columns(1, real, imag, col_band, behind, x_real, x_imag)
    next_before = lax.ppermute(right, "col", chain(col_devices, 1))
    x_real, x_imag = middle_columns(real, imag, col_band, x_real, x_imag)
    top, bottom = jnp.stack([x_real[:G], x_imag[:G]]), jnp.stack([x_real[-G:], x_imag[-G:]])
    above, below = swap_row_rims(top, bottom)

    scale = -0.5 * STEP_TIME * STEP_TIME
    new_real, new_imag = inner(x_real, x_imag, row_band, col_band, real, imag)
    new_real, new_imag = row_edges(new_real, new_imag, above, below, row_edge_band, scale)
    new_real, new_imag = col_edges(
        new_real, new_imag, (next_before, next_after, None), col_edge_band, scale, use, (0, 1, groups), False
    )
    return new_real, new_imag


def solution(mesh):
    in_specs = (P("row", "col"), P("row", "col"), P("row", None), P("row", None))
    out_specs = (P("row", "col"), P("row", "col"))
    return jax.shard_map(shards, mesh=mesh, in_specs=in_specs, out_specs=out_specs, check_vma=False)
```

```python
import functools

import jax
import jax.numpy as jnp
from jax import lax
from jax.experimental import pallas as pl
from jax.experimental.pallas import tpu as pltpu
from jax.sharding import PartitionSpec as P

BS = 128
KB = 2
G = KB * BS
STEP_TIME = 0.3
F32 = jnp.float32
BF16 = jnp.bfloat16


def split(x):
    high = x.astype(BF16)
    low = (x - high.astype(F32)).astype(BF16)
    return high, low


def dot(a, b):
    return jnp.dot(a, b, preferred_element_type=F32)


def three(a_high, a_low, b_high, b_low):
    return dot(
        jnp.concatenate([a_high, a_low, a_high], axis=1),
        jnp.concatenate([b_high, b_high, b_low], axis=0),
    )


def band_kernel(transposed, u_ref, high_ref, low_ref):
    g = pl.program_id(0)
    first = pl.multiple_of(g * G, G)

    def upper(block, d):
        return u_ref[pl.ds(first + block * BS, BS), d * BS : (d + 1) * BS]

    for i in range(KB):
        for j in range(3 * KB):
            distance = (j - KB) - i
            if distance == 0:
                diag = upper(KB + i, 0)
                value = 0.5 * (diag + diag.T)
            elif 0 < distance <= KB:
                value = upper(KB + i, distance)
                value = value.T if transposed else value
            elif -KB <= distance < 0:
                value = upper(j, -distance)
                value = value if transposed else value.T
            else:
                value = jnp.zeros((BS, BS), F32)
            high, low = split(value)
            if transposed:
                at = (0, pl.ds(j * BS, BS), pl.ds(i * BS, BS))
            else:
                slot = lax.rem(g + 2 + j // KB, 3)
                column = pl.multiple_of(slot * G + (j % KB) * BS, BS)
                at = (0, pl.ds(i * BS, BS), pl.ds(column, BS))
            high_ref[at] = high
            low_ref[at] = low


def band_groups(u_ext, transposed):
    groups = u_ext.shape[0] // G - 1
    shape = (3 * G, G) if transposed else (G, 3 * G)
    out = jax.ShapeDtypeStruct((groups,) + shape, BF16)
    block = pl.BlockSpec((1,) + shape, lambda g: (g, 0, 0))
    return pl.pallas_call(
        functools.partial(band_kernel, transposed),
        grid=(groups,),
        in_specs=[pl.BlockSpec(u_ext.shape, lambda g: (0, 0))],
        out_specs=[block, block],
        out_shape=[out, out],
        compiler_params=pltpu.CompilerParams(vmem_limit_bytes=40 << 20),
        name="band_cols" if transposed else "band_rows",
    )(u_ext)


def load_ring(t, groups, p_ref, q_ref, ring):
    ph, pl_, qh, ql = ring
    slot = lax.rem(t, 3)

    @pl.when(t == 0)
    def _():
        for ref in ring:
            ref[2] = jnp.zeros(ref.shape[1:], BF16)

    @pl.when(t < groups)
    def _():
        ph[slot], pl_[slot] = split(p_ref[...])
        qh[slot], ql[slot] = split(q_ref[...])

    @pl.when(t == groups)
    def _():
        for ref in ring:
            ref[slot] = jnp.zeros(ref.shape[1:], BF16)


def left_product(both, xh, xl, at):
    w = dot(both, xh[:, :, at].reshape(3 * G, G))
    return w[:G] + w[G:] + dot(both[:G], xl[:, :, at].reshape(3 * G, G))


def right_product(lhs, n, columns, ch_ref, cl_ref):
    lo, hi = max(n - 1, 0) * G, min(n + 2, columns) * G
    k0 = lo - (n - 1) * G
    rows = lhs(slice(lo, hi))
    band = slice(k0, k0 + hi - lo)
    return three(rows[: 2 * G], rows[2 * G :], ch_ref[n, band, :], cl_ref[n, band, :])


def left_kernel(groups, p_ref, hh_ref, hl_ref, po_ref, high, low):
    t = pl.program_id(0)
    slot = lax.rem(t, 3)

    @pl.when(t == 0)
    def _():
        for ref in (high, low):
            ref[2] = jnp.zeros(ref.shape[1:], BF16)

    @pl.when(t < groups)
    def _():
        high[slot], low[slot] = split(p_ref[...])

    @pl.when(t == groups)
    def _():
        for ref in (high, low):
            ref[slot] = jnp.zeros(ref.shape[1:], BF16)

    @pl.when(t > 0)
    def _():
        both = jnp.concatenate([hh_ref[0], hl_ref[0]], axis=0)
        for n in range(high.shape[2] // G):
            at = slice(n * G, (n + 1) * G)
            po_ref[:, at] = left_product(both, high, low, at)


def outer_kernel(side, p_ref, q_ref, h_ref, l_ref, halo_ref, pi_ref, qi_ref,
                 po_ref, qo_ref, rim_ref, rows):
    height = p_ref.shape[0]
    tile_at, halo_at = (slice(G, 3 * G), slice(0, 2 * G)), (slice(0, G), slice(2 * G, 3 * G))

    for k, x_ref in enumerate((p_ref, q_ref)):
        for half, value in enumerate(split(x_ref[...])):
            rows[k + 2 * half, :, tile_at[side]] = value
        for half, value in enumerate(split(halo_ref[k])):
            rows[k + 2 * half, :, halo_at[side]] = value
    high = rows[:2].reshape(2 * height, 3 * G)
    low = rows[2:].reshape(2 * height, 3 * G)
    right = three(high, low, h_ref[0], l_ref[0])
    p = pi_ref[...] - right[:height]
    q = qi_ref[...] - right[height:]
    po_ref[...] = p
    qo_ref[...] = q
    rim_ref[0], rim_ref[1] = p, q


def outer_columns(side, p, q, col_band, halo, p_left, q_left):
    height, width = p.shape
    rows = min(height, 2 * G)
    count, columns = height // rows, width // G
    band = pl.BlockSpec((1, 3 * G, G), lambda i: (side * (columns - 1), 0, 0))
    wide = pl.BlockSpec((rows, 2 * G), lambda i: (i, side * (columns // 2 - 1)))
    tile = pl.BlockSpec((rows, G), lambda i: (i, side * (columns - 1)))
    rim = pl.BlockSpec((2, rows, G), lambda i: (0, i, 0))
    out = jax.ShapeDtypeStruct(p.shape, F32)
    return pl.pallas_call(
        functools.partial(outer_kernel, side),
        grid=(count,),
        in_specs=[wide, wide, band, band, rim, tile, tile],
        out_specs=[tile, tile, rim],
        out_shape=[out, out, jax.ShapeDtypeStruct(halo.shape, F32)],
        input_output_aliases={5: 0, 6: 1},
        scratch_shapes=[pltpu.VMEM((4, rows, 3 * G), BF16)],
        compiler_params=pltpu.CompilerParams(vmem_limit_bytes=56 << 20),
        cost_estimate=pl.CostEstimate(flops=0, bytes_accessed=0, transcendentals=0),
        name="outer_columns",
    )(p, q, *col_band, halo, p_left, q_left)


def middle_kernel(columns, p_ref, q_ref, ch_ref, cl_ref, pi_ref, qi_ref, po_ref, qo_ref, rows):
    n = pl.program_id(1)
    height = p_ref.shape[0]

    @pl.when(n == 0)
    def _():
        for k, x_ref in enumerate((p_ref, q_ref)):
            rows[k], rows[k + 2] = split(x_ref[...])

    def product(at):
        window = slice((at - 1) * G, (at + 2) * G)
        high = rows[:2, :, window].reshape(2 * height, 3 * G)
        low = rows[2:, :, window].reshape(2 * height, 3 * G)
        right = three(high, low, ch_ref[at], cl_ref[at])
        po_ref[...] = pi_ref[...] - right[:height]
        qo_ref[...] = qi_ref[...] - right[height:]

    for at in range(1, columns - 1):
        pl.when(n == at - 1)(functools.partial(product, at))


def middle_columns(p, q, col_band, p_left, q_left):
    height, width = p.shape
    columns = width // G
    if columns <= 2:
        return p_left, q_left
    rows = min(height, 2 * G)
    whole = pl.BlockSpec((rows, width), lambda i, n: (i, 0))
    band = pl.BlockSpec(col_band[0].shape, lambda i, n: (0, 0, 0))
    tile = pl.BlockSpec((rows, G), lambda i, n: (i, n + 1))
    out = jax.ShapeDtypeStruct(p.shape, F32)
    return pl.pallas_call(
        functools.partial(middle_kernel, columns),
        grid=(height // rows, columns - 2),
        in_specs=[whole, whole, band, band, tile, tile],
        out_specs=[tile, tile],
        out_shape=[out, out],
        input_output_aliases={4: 0, 5: 1},
        scratch_shapes=[pltpu.VMEM((4, rows, width), BF16)],
        compiler_params=pltpu.CompilerParams(vmem_limit_bytes=56 << 20),
        cost_estimate=pl.CostEstimate(flops=0, bytes_accessed=0, transcendentals=0),
        name="middle_columns",
    )(p, q, *col_band, p_left, q_left)


def last_kernel(groups, p_ref, q_ref, hh_ref, hl_ref, ch_ref, cl_ref, pf_ref, qf_ref, a_ref, b_ref,
                po_ref, qo_ref, *ring):
    t = pl.program_id(0)
    load_ring(t, groups, p_ref, q_ref, ring)

    @pl.when(t > 0)
    def _():
        ph, pl_, qh, ql = ring
        mid = lax.rem(t + 2, 3)
        columns = ph.shape[2] // G
        both = jnp.concatenate([hh_ref[0], hl_ref[0]], axis=0)
        for n in range(columns):
            at = slice(n * G, (n + 1) * G)
            right = right_product(
                lambda w: jnp.concatenate([x[mid, :, w] for x in (ph, qh, pl_, ql)], axis=0),
                n, columns, ch_ref, cl_ref,
            )
            half_square = 0.5 * STEP_TIME * STEP_TIME
            slope = left_product(both, ph, pl_, at) - right[:G]
            po_ref[:, at] = a_ref[:, at] + STEP_TIME * qf_ref[:, at] - half_square * slope
            slope = left_product(both, qh, ql, at) - right[G:]
            qo_ref[:, at] = b_ref[:, at] - STEP_TIME * pf_ref[:, at] - half_square * slope


def ring_specs(p, groups):
    width = p.shape[1]
    ahead = pl.BlockSpec((G, width), lambda t: (jnp.minimum(t, groups - 1), 0))
    behind = pl.BlockSpec((G, width), lambda t: (jnp.maximum(t - 1, 0), 0))
    band = pl.BlockSpec((1, G, 3 * G), lambda t: (jnp.maximum(t - 1, 0), 0, 0))
    return ahead, behind, band, [pltpu.VMEM((3, G, width), BF16)] * 4


def from_left(p, row_band):
    groups = p.shape[0] // G
    ahead, behind, band, ring = ring_specs(p, groups)
    return pl.pallas_call(
        functools.partial(left_kernel, groups),
        grid=(groups + 1,),
        in_specs=[ahead, band, band],
        out_specs=behind,
        out_shape=jax.ShapeDtypeStruct(p.shape, F32),
        scratch_shapes=ring[:2],
        compiler_params=pltpu.CompilerParams(vmem_limit_bytes=56 << 20),
        cost_estimate=pl.CostEstimate(flops=0, bytes_accessed=0, transcendentals=0),
        name="from_left",
    )(p, *row_band)


def inner(p, q, row_band, col_band, a, b):
    groups = p.shape[0] // G
    ahead, behind, band, ring = ring_specs(p, groups)
    whole = pl.BlockSpec(col_band[0].shape, lambda t: (0, 0, 0))
    out = jax.ShapeDtypeStruct(p.shape, F32)
    return pl.pallas_call(
        functools.partial(last_kernel, groups),
        grid=(groups + 1,),
        in_specs=[ahead, ahead, band, band, whole, whole] + [behind] * 4,
        out_specs=[behind, behind],
        out_shape=[out, out],
        scratch_shapes=ring,
        compiler_params=pltpu.CompilerParams(vmem_limit_bytes=56 << 20),
        cost_estimate=pl.CostEstimate(flops=0, bytes_accessed=0, transcendentals=0),
        name="inner",
    )(p, q, *row_band, *col_band, p, q, a, b)


def row_edge_kernel(scale, h_ref, l_ref, above_ref, below_ref, p_ref, q_ref, *refs):
    outs, rims = (refs[1:3], refs[3:]) if len(refs) > 2 else (refs, ())
    high, low = h_ref[0], l_ref[0]
    both = jnp.concatenate([high, low], axis=0)

    def add(halo_ref):
        for k, (x_ref, o_ref) in enumerate(zip((p_ref, q_ref), outs)):
            xh, xl = split(halo_ref[k])
            w = dot(both, xh)
            value = x_ref[...] + scale * (w[:G] + w[G:] + dot(high, xl))
            o_ref[...] = value
            for rim in rims:
                rim[k] = value[:, :G]

    pl.when(pl.program_id(0) == 0)(lambda: add(above_ref))
    pl.when(pl.program_id(0) == 1)(lambda: add(below_ref))


def row_edges(p, q, above, below, edge_band, scale, rims=()):
    height, width = p.shape
    groups = height // G
    band = pl.BlockSpec((1, G, G), lambda s: (s, 0, 0))
    halo = pl.BlockSpec(above.shape, lambda s: (0, 0, 0))
    tile = pl.BlockSpec((G, width), lambda s: (s * (groups - 1), 0))
    rim = pl.BlockSpec((2, G, G), lambda s: (0, s * (groups - 1), 0))
    out = jax.ShapeDtypeStruct(p.shape, F32)
    return pl.pallas_call(
        functools.partial(row_edge_kernel, scale),
        grid=(2,),
        in_specs=[band, band, halo, halo, tile, tile] + [rim for _ in rims],
        out_specs=[tile, tile] + [rim for _ in rims],
        out_shape=[out, out] + [jax.ShapeDtypeStruct(x.shape, F32) for x in rims],
        input_output_aliases={4 + k: k for k in range(2 + len(rims))},
        compiler_params=pltpu.CompilerParams(vmem_limit_bytes=40 << 20),
        name="row_edges",
    )(*edge_band, above, below, p, q, *rims)


def col_edge_kernel(scale, relayed, with_rim, use_ref, *refs):
    h_ref, l_ref, before_ref, after_ref = refs[:4]
    refs = refs[4:]
    if relayed:
        extra_ref, refs = refs[0], refs[1:]
    p_ref, q_ref, po_ref, qo_ref = refs[:4]
    rim = refs[4:]
    s = pl.program_id(0)
    high, low = h_ref[0], l_ref[0]

    def add(halo_ref, side):
        rows = halo_ref.shape[1]
        halo = halo_ref[...].reshape(2 * rows, G)
        if relayed:
            halo = jnp.where(use_ref[side] > 0, extra_ref[...].reshape(2 * rows, G), halo)
        xh, xl = split(halo)
        w = dot(jnp.concatenate([xh, xl], axis=0), high)
        w = w[: 2 * rows] + w[2 * rows :] + dot(xh, low)
        for k, (x_ref, o_ref) in enumerate(((p_ref, po_ref), (q_ref, qo_ref))):
            value = x_ref[...] - scale * w[k * rows : (k + 1) * rows]
            o_ref[...] = value
            if with_rim:
                rim[side][k] = value

    pl.when(s == 0)(lambda: add(before_ref, 0))
    pl.when(s == 1)(lambda: add(after_ref, 1))


def col_edges(p, q, halos, edge_band, scale, use, groups, with_rim):
    before, after, extra = halos
    width = p.shape[1]
    first, step, count = groups
    columns = width // G
    rows = G
    if first == 0 and step == 1:
        rows = before.shape[1] // 4
        count = 4
    band = pl.BlockSpec((1, G, G), lambda s, i, use: (s, 0, 0))
    tile = pl.BlockSpec((rows, G), lambda s, i, use: (first + i * step, s * (columns - 1)))
    left = pl.BlockSpec((2, rows, G), lambda s, i, use: (0, jnp.where(s == 0, i, count - 1), 0))
    right = pl.BlockSpec((2, rows, G), lambda s, i, use: (0, jnp.where(s == 0, 0, i), 0))
    other = pl.BlockSpec((2, rows, G), lambda s, i, use: (0, i * use[s], 0))
    relayed = extra is not None
    out = jax.ShapeDtypeStruct(p.shape, F32)
    rim = jax.ShapeDtypeStruct(before.shape, F32)
    base = 5 + relayed
    return pl.pallas_call(
        functools.partial(col_edge_kernel, scale, relayed, with_rim),
        grid_spec=pltpu.PrefetchScalarGridSpec(
            num_scalar_prefetch=1,
            grid=(2, count),
            in_specs=[band, band, left, right] + [other] * relayed + [tile, tile],
            out_specs=[tile, tile] + ([left, right] if with_rim else []),
        ),
        out_shape=[out, out] + ([rim, rim] if with_rim else []),
        input_output_aliases={base: 0, base + 1: 1},
        compiler_params=pltpu.CompilerParams(vmem_limit_bytes=40 << 20),
        name="col_edges",
    )(use, *edge_band, before, after, *([extra] if relayed else []), p, q)


def chain(devices, by):
    return [(i, i + by) for i in range(devices) if 0 <= i + by < devices]


def swap_row_rims(top, bottom):
    devices = lax.axis_size("row")
    above = lax.ppermute(bottom, "row", chain(devices, 1))
    below = lax.ppermute(top, "row", chain(devices, -1))
    return above, below


def swap_col_rims(left, right, relayed):
    devices = lax.axis_size("col")
    half = devices // 2
    up, down = chain(devices, 1), chain(devices, -1)
    extra = None
    if relayed:
        up.remove((half - 1, half))
        down.remove((half, half - 1))
        mine = jnp.where(lax.axis_index("col") == half - 1, right, left)
        there = lax.ppermute(mine, "col", [(half - 1, devices - 1), (half, 0)])
    before = lax.ppermute(right, "col", up)
    after = lax.ppermute(left, "col", down)
    if relayed:
        extra = lax.ppermute(there, "col", [(devices - 1, half), (0, half - 1)])
    return before, after, extra


def masked_rows(upper_band, pattern, first_block, block_total):
    height, width = upper_band.shape
    count = height // BS
    block = first_block + jnp.arange(count, dtype=jnp.int32)
    offset = lax.broadcasted_iota(jnp.int32, (count, BS, width), 2) // BS
    factor = jnp.ones((count, BS, width), F32)
    for d in range(1, KB + 1):
        present = (pattern[:, d - 1] > 0) & (block + d < block_total)
        factor = jnp.where(offset == d, present.astype(F32)[:, None, None], factor)
    return (upper_band.reshape(count, BS, width) * factor).reshape(height, width)


def spread(value, axis, source):
    kept = jnp.where(lax.axis_index(axis) == source, value, 0).astype(value.dtype)
    return lax.psum(kept, axis)


def after(first, *values):
    return lax.optimization_barrier((first, *values))[1:]


def column_panel(panel, width, meanwhile, ahead):
    row_devices, col_devices = lax.axis_size("row"), lax.axis_size("col")
    row, col = lax.axis_index("row"), lax.axis_index("col")
    per_row = col_devices // row_devices
    if (row_devices, col_devices) != (4, 8):
        source = col // per_row
        whole = spread(panel, "row", source)
        return lax.dynamic_slice_in_dim(whole, (col - source * per_row) * width, width + G, 0), panel, panel[:G], panel
    y, x, k = col // 4, (col // 2) % 2, col % 2
    rows = (width + G) // 2
    (own,) = after(ahead, lax.dynamic_slice_in_dim(panel, k * width + y * rows, rows, 0))
    cols = lambda side: [c for c in range(col_devices) if (c // 2) % 2 == side]
    pairs = lambda hops: [
        (r * col_devices + c, t * col_devices + c) for side, r, t in hops for c in cols(side)
    ]
    both = ("row", "col")
    far = lax.ppermute(own, both, pairs([(0, 0, 2), (0, 2, 0), (1, 1, 3), (1, 3, 1)]))
    up = lax.ppermute(own, both, pairs([(0, 0, 1), (0, 2, 3), (1, 1, 2)]))
    down = lax.ppermute(own, both, pairs([(0, 2, 1), (1, 1, 0), (1, 3, 2)]))
    far, up, down = after(meanwhile, far, up, down)
    last = lax.ppermute(far, both, pairs([(0, 2, 3), (1, 1, 0)]))
    at = row - x
    low = jnp.where(at == -1, down, jnp.where(at == 0, own, jnp.where(at == 1, up, jnp.where((at == 2), far, last))))
    high = jnp.where(at == 2, own, jnp.where(at == 1, down, jnp.where(at == 3, up, jnp.where(at == 0, far, last))))
    mine, other = jnp.where(y == 0, low, high), jnp.where(y == 0, high, low)
    got = lax.ppermute(other, "col", [(c, (c + 4) % 8) for c in range(8)])
    parts = [jnp.where(y == 0, mine, got), jnp.where(y == 0, got, mine)]
    return jnp.concatenate(parts, axis=0), other, own, far


def shards(dens_real, dens_imag, upper_band, pattern):
    height, width = dens_real.shape
    row_blocks = height // BS
    row_devices, col_devices = lax.axis_size("row"), lax.axis_size("col")
    row, col = lax.axis_index("row"), lax.axis_index("col")
    first, total = row * row_blocks, row_blocks * row_devices
    tail = masked_rows(upper_band[-G:], pattern[-KB:], first + row_blocks - KB, total)
    above = lax.ppermute(tail[:, BS:], "row", chain(row_devices, 1))
    masked = masked_rows(upper_band, pattern, first, total)
    panel = jnp.concatenate([jnp.pad(above, ((0, 0), (BS, 0))), masked], axis=0)
    row_band = band_groups(panel, False)
    real, imag = dens_real, dens_imag
    x_real = from_left(real, row_band)
    rim_left = jnp.stack([x[:, :G] for x in (real, imag)])
    rim_right = jnp.stack([x[:, -G:] for x in (real, imag)])
    own_panel, landed, own_part, began = column_panel(panel, width, x_real, (rim_left, rim_right))
    x_imag = from_left(*after(began, imag), row_band)
    col_band = band_groups(own_panel, True)

    groups, columns = height // G, width // G
    slot_above, slot_below = 2, groups % 3

    def row_edge(x):
        return jnp.stack(
            [
                x[0, :, slot_above * G : (slot_above + 1) * G],
                x[groups - 1, :, slot_below * G : (slot_below + 1) * G],
            ]
        )

    def col_edge(x):
        return jnp.stack([x[0, :G], x[columns - 1, 2 * G :]])

    row_edge_band = [row_edge(x) for x in row_band]
    col_edge_band = [col_edge(x) for x in col_band]
    half = col_devices // 2
    use = jnp.stack([col == half, col == half - 1]).astype(jnp.int32)

    before, behind, _ = swap_col_rims(rim_left, rim_right, False)
    top, bottom = jnp.stack([real[:G], imag[:G]]), jnp.stack([real[-G:], imag[-G:]])
    above, below = swap_row_rims(*after(landed, top, bottom))
    x_real, x_imag, left = outer_columns(0, real, imag, col_band, before, x_real, x_imag)
    x_real, x_imag, left = row_edges(
        x_real, x_imag, above, below, row_edge_band, 1.0, (left,)
    )
    next_after = lax.ppermute(left, "col", chain(col_devices, -1))
    x_real, x_imag, right = outer_columns(1, real, imag, col_band, behind, x_real, x_imag)
    next_before = lax.ppermute(right, "col", chain(col_devices, 1))
    x_real, x_imag = middle_columns(real, imag, col_band, x_real, x_imag)
    top, bottom = jnp.stack([x_real[:G], x_imag[:G]]), jnp.stack([x_real[-G:], x_imag[-G:]])
    above, below = swap_row_rims(top, bottom)

    scale = -0.5 * STEP_TIME * STEP_TIME
    new_real, new_imag = inner(x_real, x_imag, row_band, col_band, real, imag)
    new_real, new_imag = row_edges(new_real, new_imag, above, below, row_edge_band, scale)
    new_real, new_imag = col_edges(
        new_real, new_imag, (next_before, next_after, None), col_edge_band, scale, use, (0, 1, groups), False
    )
    return new_real, new_imag


def solution(mesh):
    in_specs = (P("row", "col"), P("row", "col"), P("row", None), P("row", None))
    out_specs = (P("row", "col"), P("row", "col"))
    return jax.shard_map(shards, mesh=mesh, in_specs=in_specs, out_specs=out_specs, check_vma=False)
```

```python
import functools

import jax
import jax.numpy as jnp
from jax import lax
from jax.experimental import pallas as pl
from jax.experimental.pallas import tpu as pltpu
from jax.sharding import PartitionSpec as P

BS = 128
KB = 2
G = KB * BS
STEP_TIME = 0.3
F32 = jnp.float32
BF16 = jnp.bfloat16


def split(x):
    high = x.astype(BF16)
    low = (x - high.astype(F32)).astype(BF16)
    return high, low


def dot(a, b):
    return jnp.dot(a, b, preferred_element_type=F32)


def three(a_high, a_low, b_high, b_low):
    return dot(
        jnp.concatenate([a_high, a_low, a_high], axis=1),
        jnp.concatenate([b_high, b_high, b_low], axis=0),
    )


def band_kernel(transposed, u_ref, high_ref, low_ref):
    g = pl.program_id(0)
    first = pl.multiple_of(g * G, G)

    def upper(block, d):
        return u_ref[pl.ds(first + block * BS, BS), d * BS : (d + 1) * BS]

    for i in range(KB):
        for j in range(3 * KB):
            distance = (j - KB) - i
            if distance == 0:
                diag = upper(KB + i, 0)
                value = 0.5 * (diag + diag.T)
            elif 0 < distance <= KB:
                value = upper(KB + i, distance)
                value = value.T if transposed else value
            elif -KB <= distance < 0:
                value = upper(j, -distance)
                value = value if transposed else value.T
            else:
                value = jnp.zeros((BS, BS), F32)
            high, low = split(value)
            if transposed:
                at = (0, pl.ds(j * BS, BS), pl.ds(i * BS, BS))
            else:
                slot = lax.rem(g + 2 + j // KB, 3)
                column = pl.multiple_of(slot * G + (j % KB) * BS, BS)
                at = (0, pl.ds(i * BS, BS), pl.ds(column, BS))
            high_ref[at] = high
            low_ref[at] = low


def band_groups(u_ext, transposed):
    groups = u_ext.shape[0] // G - 1
    shape = (3 * G, G) if transposed else (G, 3 * G)
    out = jax.ShapeDtypeStruct((groups,) + shape, BF16)
    block = pl.BlockSpec((1,) + shape, lambda g: (g, 0, 0))
    return pl.pallas_call(
        functools.partial(band_kernel, transposed),
        grid=(groups,),
        in_specs=[pl.BlockSpec(u_ext.shape, lambda g: (0, 0))],
        out_specs=[block, block],
        out_shape=[out, out],
        compiler_params=pltpu.CompilerParams(vmem_limit_bytes=40 << 20),
        name="band_cols" if transposed else "band_rows",
    )(u_ext)


def load_ring(t, groups, p_ref, q_ref, ring):
    ph, pl_, qh, ql = ring
    slot = lax.rem(t, 3)

    @pl.when(t == 0)
    def _():
        for ref in ring:
            ref[2] = jnp.zeros(ref.shape[1:], BF16)

    @pl.when(t < groups)
    def _():
        ph[slot], pl_[slot] = split(p_ref[...])
        qh[slot], ql[slot] = split(q_ref[...])

    @pl.when(t == groups)
    def _():
        for ref in ring:
            ref[slot] = jnp.zeros(ref.shape[1:], BF16)


def left_product(both, xh, xl, at):
    w = dot(both, xh[:, :, at].reshape(3 * G, G))
    return w[:G] + w[G:] + dot(both[:G], xl[:, :, at].reshape(3 * G, G))


def right_product(lhs, n, columns, ch_ref, cl_ref):
    lo, hi = max(n - 1, 0) * G, min(n + 2, columns) * G
    k0 = lo - (n - 1) * G
    rows = lhs(slice(lo, hi))
    band = slice(k0, k0 + hi - lo)
    return three(rows[: 2 * G], rows[2 * G :], ch_ref[n, band, :], cl_ref[n, band, :])


def left_kernel(groups, p_ref, hh_ref, hl_ref, po_ref, high, low):
    t = pl.program_id(0)
    slot = lax.rem(t, 3)

    @pl.when(t == 0)
    def _():
        for ref in (high, low):
            ref[2] = jnp.zeros(ref.shape[1:], BF16)

    @pl.when(t < groups)
    def _():
        high[slot], low[slot] = split(p_ref[...])

    @pl.when(t == groups)
    def _():
        for ref in (high, low):
            ref[slot] = jnp.zeros(ref.shape[1:], BF16)

    @pl.when(t > 0)
    def _():
        both = jnp.concatenate([hh_ref[0], hl_ref[0]], axis=0)
        for n in range(high.shape[2] // G):
            at = slice(n * G, (n + 1) * G)
            po_ref[:, at] = left_product(both, high, low, at)


def outer_kernel(side, p_ref, q_ref, h_ref, l_ref, halo_ref, pi_ref, qi_ref,
                 po_ref, qo_ref, rim_ref, rows):
    height = p_ref.shape[0]
    tile_at, halo_at = (slice(G, 3 * G), slice(0, 2 * G)), (slice(0, G), slice(2 * G, 3 * G))

    for k, x_ref in enumerate((p_ref, q_ref)):
        for half, value in enumerate(split(x_ref[...])):
            rows[k + 2 * half, :, tile_at[side]] = value
        for half, value in enumerate(split(halo_ref[k])):
            rows[k + 2 * half, :, halo_at[side]] = value
    high = rows[:2].reshape(2 * height, 3 * G)
    low = rows[2:].reshape(2 * height, 3 * G)
    right = three(high, low, h_ref[0], l_ref[0])
    p = pi_ref[...] - right[:height]
    q = qi_ref[...] - right[height:]
    po_ref[...] = p
    qo_ref[...] = q
    rim_ref[0], rim_ref[1] = p, q


def outer_columns(side, p, q, col_band, halo, p_left, q_left):
    height, width = p.shape
    rows = min(height, 2 * G)
    count, columns = height // rows, width // G
    band = pl.BlockSpec((1, 3 * G, G), lambda i: (side * (columns - 1), 0, 0))
    wide = pl.BlockSpec((rows, 2 * G), lambda i: (i, side * (columns // 2 - 1)))
    tile = pl.BlockSpec((rows, G), lambda i: (i, side * (columns - 1)))
    rim = pl.BlockSpec((2, rows, G), lambda i: (0, i, 0))
    out = jax.ShapeDtypeStruct(p.shape, F32)
    return pl.pallas_call(
        functools.partial(outer_kernel, side),
        grid=(count,),
        in_specs=[wide, wide, band, band, rim, tile, tile],
        out_specs=[tile, tile, rim],
        out_shape=[out, out, jax.ShapeDtypeStruct(halo.shape, F32)],
        input_output_aliases={5: 0, 6: 1},
        scratch_shapes=[pltpu.VMEM((4, rows, 3 * G), BF16)],
        compiler_params=pltpu.CompilerParams(vmem_limit_bytes=56 << 20),
        cost_estimate=pl.CostEstimate(flops=0, bytes_accessed=0, transcendentals=0),
        name="outer_columns",
    )(p, q, *col_band, halo, p_left, q_left)


def middle_kernel(columns, p_ref, q_ref, ch_ref, cl_ref, pi_ref, qi_ref, po_ref, qo_ref, rows):
    for k, x_ref in enumerate((p_ref, q_ref)):
        rows[k], rows[k + 2] = split(x_ref[...])
    for n in range(1, columns - 1):
        at = slice((n - 1) * G, n * G)
        right = right_product(
            lambda w: rows[:, :, w].reshape(4 * G, w.stop - w.start), n, columns, ch_ref, cl_ref
        )
        po_ref[:, at] = pi_ref[:, at] - right[:G]
        qo_ref[:, at] = qi_ref[:, at] - right[G:]


def middle_columns(p, q, col_band, p_left, q_left):
    height, width = p.shape
    columns = width // G
    if columns <= 2:
        return p_left, q_left
    whole = pl.BlockSpec((G, width), lambda i: (i, 0))
    band = pl.BlockSpec(col_band[0].shape, lambda i: (0, 0, 0))
    tile = pl.BlockSpec((pl.Element(G), pl.Element(width - 2 * G)), lambda i: (i * G, G))
    out = jax.ShapeDtypeStruct(p.shape, F32)
    return pl.pallas_call(
        functools.partial(middle_kernel, columns),
        grid=(height // G,),
        in_specs=[whole, whole, band, band, tile, tile],
        out_specs=[tile, tile],
        out_shape=[out, out],
        input_output_aliases={4: 0, 5: 1},
        scratch_shapes=[pltpu.VMEM((4, G, width), BF16)],
        compiler_params=pltpu.CompilerParams(vmem_limit_bytes=56 << 20),
        cost_estimate=pl.CostEstimate(flops=0, bytes_accessed=0, transcendentals=0),
        name="middle_columns",
    )(p, q, *col_band, p_left, q_left)


def last_kernel(groups, p_ref, q_ref, hh_ref, hl_ref, ch_ref, cl_ref, pf_ref, qf_ref, a_ref, b_ref,
                po_ref, qo_ref, *ring):
    t = pl.program_id(0)
    load_ring(t, groups, p_ref, q_ref, ring)

    @pl.when(t > 0)
    def _():
        ph, pl_, qh, ql = ring
        mid = lax.rem(t + 2, 3)
        columns = ph.shape[2] // G
        both = jnp.concatenate([hh_ref[0], hl_ref[0]], axis=0)
        for n in range(columns):
            at = slice(n * G, (n + 1) * G)
            right = right_product(
                lambda w: jnp.concatenate([x[mid, :, w] for x in (ph, qh, pl_, ql)], axis=0),
                n, columns, ch_ref, cl_ref,
            )
            half_square = 0.5 * STEP_TIME * STEP_TIME
            slope = left_product(both, ph, pl_, at) - right[:G]
            po_ref[:, at] = a_ref[:, at] + STEP_TIME * qf_ref[:, at] - half_square * slope
            slope = left_product(both, qh, ql, at) - right[G:]
            qo_ref[:, at] = b_ref[:, at] - STEP_TIME * pf_ref[:, at] - half_square * slope


def ring_specs(p, groups):
    width = p.shape[1]
    ahead = pl.BlockSpec((G, width), lambda t: (jnp.minimum(t, groups - 1), 0))
    behind = pl.BlockSpec((G, width), lambda t: (jnp.maximum(t - 1, 0), 0))
    band = pl.BlockSpec((1, G, 3 * G), lambda t: (jnp.maximum(t - 1, 0), 0, 0))
    return ahead, behind, band, [pltpu.VMEM((3, G, width), BF16)] * 4


def from_left(p, row_band):
    groups = p.shape[0] // G
    ahead, behind, band, ring = ring_specs(p, groups)
    return pl.pallas_call(
        functools.partial(left_kernel, groups),
        grid=(groups + 1,),
        in_specs=[ahead, band, band],
        out_specs=behind,
        out_shape=jax.ShapeDtypeStruct(p.shape, F32),
        scratch_shapes=ring[:2],
        compiler_params=pltpu.CompilerParams(vmem_limit_bytes=56 << 20),
        cost_estimate=pl.CostEstimate(flops=0, bytes_accessed=0, transcendentals=0),
        name="from_left",
    )(p, *row_band)


def inner(p, q, row_band, col_band, a, b):
    groups = p.shape[0] // G
    ahead, behind, band, ring = ring_specs(p, groups)
    whole = pl.BlockSpec(col_band[0].shape, lambda t: (0, 0, 0))
    out = jax.ShapeDtypeStruct(p.shape, F32)
    return pl.pallas_call(
        functools.partial(last_kernel, groups),
        grid=(groups + 1,),
        in_specs=[ahead, ahead, band, band, whole, whole] + [behind] * 4,
        out_specs=[behind, behind],
        out_shape=[out, out],
        scratch_shapes=ring,
        compiler_params=pltpu.CompilerParams(vmem_limit_bytes=56 << 20),
        cost_estimate=pl.CostEstimate(flops=0, bytes_accessed=0, transcendentals=0),
        name="inner",
    )(p, q, *row_band, *col_band, p, q, a, b)


def row_edge_kernel(scale, h_ref, l_ref, above_ref, below_ref, p_ref, q_ref, *refs):
    outs, rims = (refs[1:3], refs[3:]) if len(refs) > 2 else (refs, ())
    high, low = h_ref[0], l_ref[0]
    both = jnp.concatenate([high, low], axis=0)

    def add(halo_ref):
        for k, (x_ref, o_ref) in enumerate(zip((p_ref, q_ref), outs)):
            xh, xl = split(halo_ref[k])
            w = dot(both, xh)
            value = x_ref[...] + scale * (w[:G] + w[G:] + dot(high, xl))
            o_ref[...] = value
            for rim in rims:
                rim[k] = value[:, :G]

    pl.when(pl.program_id(0) == 0)(lambda: add(above_ref))
    pl.when(pl.program_id(0) == 1)(lambda: add(below_ref))


def row_edges(p, q, above, below, edge_band, scale, rims=()):
    height, width = p.shape
    groups = height // G
    band = pl.BlockSpec((1, G, G), lambda s: (s, 0, 0))
    halo = pl.BlockSpec(above.shape, lambda s: (0, 0, 0))
    tile = pl.BlockSpec((G, width), lambda s: (s * (groups - 1), 0))
    rim = pl.BlockSpec((2, G, G), lambda s: (0, s * (groups - 1), 0))
    out = jax.ShapeDtypeStruct(p.shape, F32)
    return pl.pallas_call(
        functools.partial(row_edge_kernel, scale),
        grid=(2,),
        in_specs=[band, band, halo, halo, tile, tile] + [rim for _ in rims],
        out_specs=[tile, tile] + [rim for _ in rims],
        out_shape=[out, out] + [jax.ShapeDtypeStruct(x.shape, F32) for x in rims],
        input_output_aliases={4 + k: k for k in range(2 + len(rims))},
        compiler_params=pltpu.CompilerParams(vmem_limit_bytes=40 << 20),
        name="row_edges",
    )(*edge_band, above, below, p, q, *rims)


def col_edge_kernel(scale, relayed, with_rim, use_ref, *refs):
    h_ref, l_ref, before_ref, after_ref = refs[:4]
    refs = refs[4:]
    if relayed:
        extra_ref, refs = refs[0], refs[1:]
    p_ref, q_ref, po_ref, qo_ref = refs[:4]
    rim = refs[4:]
    s = pl.program_id(0)
    high, low = h_ref[0], l_ref[0]

    def add(halo_ref, side):
        rows = halo_ref.shape[1]
        halo = halo_ref[...].reshape(2 * rows, G)
        if relayed:
            halo = jnp.where(use_ref[side] > 0, extra_ref[...].reshape(2 * rows, G), halo)
        xh, xl = split(halo)
        w = dot(jnp.concatenate([xh, xl], axis=0), high)
        w = w[: 2 * rows] + w[2 * rows :] + dot(xh, low)
        for k, (x_ref, o_ref) in enumerate(((p_ref, po_ref), (q_ref, qo_ref))):
            value = x_ref[...] - scale * w[k * rows : (k + 1) * rows]
            o_ref[...] = value
            if with_rim:
                rim[side][k] = value

    pl.when(s == 0)(lambda: add(before_ref, 0))
    pl.when(s == 1)(lambda: add(after_ref, 1))


def col_edges(p, q, halos, edge_band, scale, use, groups, with_rim):
    before, after, extra = halos
    width = p.shape[1]
    first, step, count = groups
    columns = width // G
    rows = G
    if first == 0 and step == 1:
        rows = before.shape[1] // 4
        count = 4
    band = pl.BlockSpec((1, G, G), lambda s, i, use: (s, 0, 0))
    tile = pl.BlockSpec((rows, G), lambda s, i, use: (first + i * step, s * (columns - 1)))
    left = pl.BlockSpec((2, rows, G), lambda s, i, use: (0, jnp.where(s == 0, i, count - 1), 0))
    right = pl.BlockSpec((2, rows, G), lambda s, i, use: (0, jnp.where(s == 0, 0, i), 0))
    other = pl.BlockSpec((2, rows, G), lambda s, i, use: (0, i * use[s], 0))
    relayed = extra is not None
    out = jax.ShapeDtypeStruct(p.shape, F32)
    rim = jax.ShapeDtypeStruct(before.shape, F32)
    base = 5 + relayed
    return pl.pallas_call(
        functools.partial(col_edge_kernel, scale, relayed, with_rim),
        grid_spec=pltpu.PrefetchScalarGridSpec(
            num_scalar_prefetch=1,
            grid=(2, count),
            in_specs=[band, band, left, right] + [other] * relayed + [tile, tile],
            out_specs=[tile, tile] + ([left, right] if with_rim else []),
        ),
        out_shape=[out, out] + ([rim, rim] if with_rim else []),
        input_output_aliases={base: 0, base + 1: 1},
        compiler_params=pltpu.CompilerParams(vmem_limit_bytes=40 << 20),
        name="col_edges",
    )(use, *edge_band, before, after, *([extra] if relayed else []), p, q)


def chain(devices, by):
    return [(i, i + by) for i in range(devices) if 0 <= i + by < devices]


def swap_row_rims(top, bottom):
    devices = lax.axis_size("row")
    above = lax.ppermute(bottom, "row", chain(devices, 1))
    below = lax.ppermute(top, "row", chain(devices, -1))
    return above, below


def swap_col_rims(left, right, relayed):
    devices = lax.axis_size("col")
    half = devices // 2
    up, down = chain(devices, 1), chain(devices, -1)
    extra = None
    if relayed:
        up.remove((half - 1, half))
        down.remove((half, half - 1))
        mine = jnp.where(lax.axis_index("col") == half - 1, right, left)
        there = lax.ppermute(mine, "col", [(half - 1, devices - 1), (half, 0)])
    before = lax.ppermute(right, "col", up)
    after = lax.ppermute(left, "col", down)
    if relayed:
        extra = lax.ppermute(there, "col", [(devices - 1, half), (0, half - 1)])
    return before, after, extra


def masked_rows(upper_band, pattern, first_block, block_total):
    height, width = upper_band.shape
    count = height // BS
    block = first_block + jnp.arange(count, dtype=jnp.int32)
    offset = lax.broadcasted_iota(jnp.int32, (count, BS, width), 2) // BS
    factor = jnp.ones((count, BS, width), F32)
    for d in range(1, KB + 1):
        present = (pattern[:, d - 1] > 0) & (block + d < block_total)
        factor = jnp.where(offset == d, present.astype(F32)[:, None, None], factor)
    return (upper_band.reshape(count, BS, width) * factor).reshape(height, width)


def spread(value, axis, source):
    kept = jnp.where(lax.axis_index(axis) == source, value, 0).astype(value.dtype)
    return lax.psum(kept, axis)


def after(first, *values):
    return lax.optimization_barrier((first, *values))[1:]


def column_panel(panel, width, meanwhile, ahead):
    row_devices, col_devices = lax.axis_size("row"), lax.axis_size("col")
    row, col = lax.axis_index("row"), lax.axis_index("col")
    per_row = col_devices // row_devices
    if (row_devices, col_devices) != (4, 8):
        source = col // per_row
        whole = spread(panel, "row", source)
        return lax.dynamic_slice_in_dim(whole, (col - source * per_row) * width, width + G, 0), panel, panel[:G], panel
    y, x, k = col // 4, (col // 2) % 2, col % 2
    rows = (width + G) // 2
    (own,) = after(ahead, lax.dynamic_slice_in_dim(panel, k * width + y * rows, rows, 0))
    cols = lambda side: [c for c in range(col_devices) if (c // 2) % 2 == side]
    pairs = lambda hops: [
        (r * col_devices + c, t * col_devices + c) for side, r, t in hops for c in cols(side)
    ]
    both = ("row", "col")
    far = lax.ppermute(own, both, pairs([(0, 0, 2), (0, 2, 0), (1, 1, 3), (1, 3, 1)]))
    up = lax.ppermute(own, both, pairs([(0, 0, 1), (0, 2, 3), (1, 1, 2)]))
    down = lax.ppermute(own, both, pairs([(0, 2, 1), (1, 1, 0), (1, 3, 2)]))
    far, up, down = after(meanwhile, far, up, down)
    last = lax.ppermute(far, both, pairs([(0, 2, 3), (1, 1, 0)]))
    at = row - x
    low = jnp.where(at == -1, down, jnp.where(at == 0, own, jnp.where(at == 1, up, jnp.where((at == 2), far, last))))
    high = jnp.where(at == 2, own, jnp.where(at == 1, down, jnp.where(at == 3, up, jnp.where(at == 0, far, last))))
    mine, other = jnp.where(y == 0, low, high), jnp.where(y == 0, high, low)
    got = lax.ppermute(other, "col", [(c, (c + 4) % 8) for c in range(8)])
    parts = [jnp.where(y == 0, mine, got), jnp.where(y == 0, got, mine)]
    return jnp.concatenate(parts, axis=0), other, own, far


def shards(dens_real, dens_imag, upper_band, pattern):
    height, width = dens_real.shape
    row_blocks = height // BS
    row_devices, col_devices = lax.axis_size("row"), lax.axis_size("col")
    row, col = lax.axis_index("row"), lax.axis_index("col")
    first, total = row * row_blocks, row_blocks * row_devices
    tail = masked_rows(upper_band[-G:], pattern[-KB:], first + row_blocks - KB, total)
    above = lax.ppermute(tail[:, BS:], "row", chain(row_devices, 1))
    masked = masked_rows(upper_band, pattern, first, total)
    panel = jnp.concatenate([jnp.pad(above, ((0, 0), (BS, 0))), masked], axis=0)
    row_band = band_groups(panel, False)
    real, imag = dens_real, dens_imag
    x_real = from_left(real, row_band)
    rim_left = jnp.stack([x[:, :G] for x in (real, imag)])
    rim_right = jnp.stack([x[:, -G:] for x in (real, imag)])
    own_panel, landed, own_part, began = column_panel(panel, width, x_real, (rim_left, rim_right))
    x_imag = from_left(*after(began, imag), row_band)
    col_band = band_groups(own_panel, True)

    groups, columns = height // G, width // G
    slot_above, slot_below = 2, groups % 3

    def row_edge(x):
        return jnp.stack(
            [
                x[0, :, slot_above * G : (slot_above + 1) * G],
                x[groups - 1, :, slot_below * G : (slot_below + 1) * G],
            ]
        )

    def col_edge(x):
        return jnp.stack([x[0, :G], x[columns - 1, 2 * G :]])

    row_edge_band = [row_edge(x) for x in row_band]
    col_edge_band = [col_edge(x) for x in col_band]
    half = col_devices // 2
    use = jnp.stack([col == half, col == half - 1]).astype(jnp.int32)

    before, behind, _ = swap_col_rims(rim_left, rim_right, False)
    top, bottom = jnp.stack([real[:G], imag[:G]]), jnp.stack([real[-G:], imag[-G:]])
    above, below = swap_row_rims(*after(landed, top, bottom))
    x_real, x_imag, left = outer_columns(0, real, imag, col_band, before, x_real, x_imag)
    x_real, x_imag, left = row_edges(
        x_real, x_imag, above, below, row_edge_band, 1.0, (left,)
    )
    next_after = lax.ppermute(left, "col", chain(col_devices, -1))
    x_real, x_imag, right = outer_columns(1, real, imag, col_band, behind, x_real, x_imag)
    next_before = lax.ppermute(right, "col", chain(col_devices, 1))
    x_real, x_imag = middle_columns(real, imag, col_band, x_real, x_imag)
    top, bottom = jnp.stack([x_real[:G], x_imag[:G]]), jnp.stack([x_real[-G:], x_imag[-G:]])
    above, below = swap_row_rims(top, bottom)

    scale = -0.5 * STEP_TIME * STEP_TIME
    new_real, new_imag = inner(x_real, x_imag, row_band, col_band, real, imag)
    new_real, new_imag = row_edges(new_real, new_imag, above, below, row_edge_band, scale)
    new_real, new_imag = col_edges(
        new_real, new_imag, (next_before, next_after, None), col_edge_band, scale, use, (0, 1, groups), False
    )
    return new_real, new_imag


def solution(mesh):
    in_specs = (P("row", "col"), P("row", "col"), P("row", None), P("row", None))
    out_specs = (P("row", "col"), P("row", "col"))
    return jax.shard_map(shards, mesh=mesh, in_specs=in_specs, out_specs=out_specs, check_vma=False)
```
